32 devices in a mesh: groups: 2 (over y), rows: 4 (over z), cols: 4 (over x, core).
Axes of the slice: x: 2, y: 2, z: 4, core: 2. Of those that a mesh axis runs over, the one named last changes fastest.
Arguments:
- positions: float32 [32, 4, 2, 1024], P(('groups', 'rows'), 'cols'), parts along dimension 0, may hold values from 0 to 1
- region_cell: int32 [32, 4], P(('groups', 'rows'), 'cols'), parts along dimension 0, may hold values from 0 to 63, as said below
- spread: float32 [32, 4, 1024], P(('groups', 'rows'), 'cols'), parts along dimension 0, may hold values from 0.4 to 0.8
- obs_var: float32 [32, 4, 1024], P(('groups', 'rows'), 'cols'), parts along dimension 0, may hold values from 1.05 to 1.6
- counts: int32 [32, 4], P(('groups', 'rows'), 'cols'), parts along dimension 0, may hold values from 1 to 1024, as said below
- pair_flags: int32 [32, 4, 16, 4], P(('groups', 'rows'), None, None, 'cols'), parts along dimension 0, may hold values from 0 to 1, as said below
- iterate: float32 [32, 4, 1024], P(('groups', 'rows'), 'cols'), parts along dimension 0, may hold values from -24 to 24
- residual: float32 [32, 4, 1024], P(('groups', 'rows'), 'cols'), parts along dimension 0, may hold values from -24 to 24
- direction: float32 [32, 4, 1024], P(('groups', 'rows'), 'cols'), parts along dimension 0, may hold values from -24 to 24
Outputs:
- iterate_next: float32 [32, 4, 1024], P(('groups', 'rows'), 'cols'), parts along dimension 0
- residual_next: float32 [32, 4, 1024], P(('groups', 'rows'), 'cols'), parts along dimension 0
- direction_next: float32 [32, 4, 1024], P(('groups', 'rows'), 'cols'), parts along dimension 0
The draws below stay inside these ranges and needn't reach their ends.
There are 2 independent parts, one for each index of `groups`. The reference program is written for one: setup_inputs(seed, part) draws one part's arguments, and reference() takes and returns one part's arrays. A program takes and returns all parts, laid end to end along the dimension named above; each array names one. Nothing has to cross between parts.
Inputs may be any that keep to these rules, and one draw needn't show every extreme that they name: `counts`: each region holds 1 to 1024 observations; some region holds exactly 1024. `region_cell`: a permutation of the 64 cells of a grid of 16 rows by 4 columns. pair_flags[a, b] is 1 exactly where the cells of regions a and b differ by at most one in row and in column; the flags are symmetric; every region lists itself; no region lists more than 9 regions, itself included, and some list exactly 9.
All inputs are finite; a program needn't handle non-finite values.
Results may differ from the reference program's by a relative error of at most 0.00002.
Values sent between devices are 32-bit elements; how exact they have to be, the bound alone decides.
A program may use at most 64 MiB of HBM per device.

```python
import math
import jax
import jax.numpy as jnp
from jax import lax

SLOT = 1024
NBR = 9
NRR = 16
NRC = 4


LOG_THREE = 1.0986122886681098


def grid_cells(key):
    cell_key = jax.random.fold_in(key, 11)
    return jax.random.permutation(cell_key, NRR * NRC).astype(jnp.int32)


def planted_pair(key):
    cells = grid_cells(key)
    row_key = jax.random.fold_in(key, 13)
    col_key = jax.random.fold_in(key, 17)
    anchor_row = jax.random.randint(row_key, (), 0, NRR - 1).astype(jnp.int32)
    anchor_col = jax.random.randint(col_key, (), 0, NRC - 1).astype(jnp.int32)
    region_index = jnp.arange(NRR * NRC, dtype=jnp.int32)
    first_cell = anchor_row * NRC + anchor_col
    second_cell = first_cell + NRC + 1
    receiver = jnp.sum(jnp.where(cells == first_cell, region_index, 0)).astype(jnp.int32)
    source = jnp.sum(jnp.where(cells == second_cell, region_index, 0)).astype(jnp.int32)
    return (receiver, source)


def rising_scale():
    shape = (NRR, NRC, SLOT)
    rows_at = lax.broadcasted_iota(jnp.float32, shape, 0) / max(NRR - 1, 1)
    cols_at = lax.broadcasted_iota(jnp.float32, shape, 1) / max(NRC - 1, 1)
    return 0.5 * jnp.exp(LOG_THREE * (rows_at + cols_at))


def plant_dipole(values, source):
    shape = (NRR * NRC, SLOT)
    clump = SLOT // 8
    region_at = lax.broadcasted_iota(jnp.int32, shape, 0)
    slot_at = lax.broadcasted_iota(jnp.int32, shape, 1)
    positive = (region_at == source) & (slot_at < clump)
    negative = (region_at == source) & (slot_at >= clump) & (slot_at < 2 * clump)
    flat = values.reshape(shape)
    flat = jnp.where(positive, 24.0, flat)
    flat = jnp.where(negative, -24.0, flat)
    return flat.reshape(NRR, NRC, SLOT)


def draw_region_cell(key, part):
    cells = grid_cells(key)
    return cells.reshape(NRR, NRC)


def draw_positions(key, part):
    receiver, source = planted_pair(key)
    key = jax.random.fold_in(key, 7)
    base_key, jitter_key = jax.random.split(key)
    shape = (NRR * NRC, 2, SLOT)
    scattered = jax.random.uniform(base_key, shape, jnp.float32, 0.0, 0.999)
    jitter = jax.random.uniform(jitter_key, shape, jnp.float32, 0.0, 0.004)
    clump = SLOT // 8
    region_at = lax.broadcasted_iota(jnp.int32, shape, 0)
    dim_at = lax.broadcasted_iota(jnp.int32, shape, 1)
    slot_at = lax.broadcasted_iota(jnp.int32, shape, 2)
    first_clump = slot_at < clump
    second_clump = (slot_at >= clump) & (slot_at < 2 * clump)
    near_corner = (region_at == receiver) & first_clump
    positive = (region_at == source) & first_clump
    negative = (region_at == source) & second_clump
    target = jnp.where(near_corner, 0.99, 0.0)
    target = jnp.where(positive, jnp.where(dim_at == 0, 0.751, 0.501), target)
    target = jnp.where(negative, jnp.where(dim_at == 0, 0.792, 0.529), target)
    planted = near_corner | positive | negative
    placed = jnp.where(planted, target + jitter, scattered)
    return placed.astype(jnp.float32).reshape(NRR, NRC, 2, SLOT)


def draw_pair_flags(key, part):
    cells = grid_cells(key)
    cells_x = cells // NRC
    cells_y = cells % NRC
    near_x = jnp.abs(cells_x[:, None] - cells_x[None, :]) <= 1
    near_y = jnp.abs(cells_y[:, None] - cells_y[None, :]) <= 1
    listed = (near_x & near_y).astype(jnp.int32)
    return listed.reshape(NRR, NRC, NRR, NRC)


def draw_counts(key, part):
    receiver, source = planted_pair(key)
    key = jax.random.fold_in(key, 5)
    base_key, pick_key = jax.random.split(key)
    base_counts = jax.random.randint(base_key, (NRR * NRC,), 1, 2 * SLOT // 3 + 1)
    chosen = jax.random.randint(pick_key, (), 0, NRR * NRC)
    region_index = jnp.arange(NRR * NRC)
    filled = jnp.where(region_index == chosen, SLOT, base_counts)
    filled = jnp.where(region_index == source, jnp.maximum(filled, SLOT // 4), filled)
    filled = jnp.where(region_index == receiver, jnp.maximum(filled, SLOT // 8), filled)
    return filled.astype(jnp.int32).reshape(NRR, NRC)


def draw_iterate(key, part):
    key = jax.random.fold_in(key, 21)
    shape = (NRR, NRC, SLOT)
    return rising_scale() * jnp.clip(jax.random.normal(key, shape, jnp.float32), -5.0, 5.0)


def draw_residual(key, part):
    key = jax.random.fold_in(key, 22)
    shape = (NRR, NRC, SLOT)
    return rising_scale() * jnp.clip(jax.random.normal(key, shape, jnp.float32), -5.0, 5.0)


def draw_direction(key, part):
    receiver, source = planted_pair(key)
    key = jax.random.fold_in(key, 23)
    shape = (NRR, NRC, SLOT)
    values = rising_scale() * jnp.clip(jax.random.normal(key, shape, jnp.float32), -5.0, 5.0)
    return plant_dipole(values, source)


def shard_levels(key, shape, cuts, smallest, high):
    level, own = 1.0, jax.random.fold_in(key, 6)
    for dim, shards_of in cuts:
        draws = jnp.exp(jax.random.uniform(jax.random.fold_in(own, dim), (shards_of,), jnp.float32, smallest / len(cuts), high / len(cuts)))
        level = level * jnp.repeat(draws, shape[dim] // shards_of).reshape([-1 if axis == dim else 1 for axis in range(len(shape))])
    return level


def setup_inputs(seed: int = 0, part: int = 0) -> dict:
    arg_keys = jax.random.split(jax.random.key(seed), 10)
    part_splits = jax.random.split(jax.random.fold_in(arg_keys[9], part), 10)
    return {
        "positions": draw_positions(jax.random.fold_in(jax.random.fold_in(arg_keys[9], part), 71), part),
        "region_cell": draw_region_cell(jax.random.fold_in(jax.random.fold_in(arg_keys[9], part), 71), part),
        "spread": jnp.clip(jnp.exp(math.log(0.8) - 0.6931472 * jax.random.uniform(part_splits[2], (NRR, NRC, SLOT), jnp.float32) ** shard_levels(part_splits[2], (NRR, NRC, SLOT), ((0, 4), (1, 4)), -0.2, 0.2)), 0.4, 0.8),
        "obs_var": jnp.clip(jnp.exp(math.log(1.6) - 0.42121353 * jax.random.uniform(part_splits[3], (NRR, NRC, SLOT), jnp.float32) ** shard_levels(part_splits[3], (NRR, NRC, SLOT), ((0, 4), (1, 4)), -0.2, 0.2)), 1.05, 1.6),
        "counts": draw_counts(jax.random.fold_in(jax.random.fold_in(arg_keys[9], part), 71), part),
        "pair_flags": draw_pair_flags(jax.random.fold_in(jax.random.fold_in(arg_keys[9], part), 71), part),
        "iterate": draw_iterate(jax.random.fold_in(jax.random.fold_in(arg_keys[9], part), 71), part),
        "residual": draw_residual(jax.random.fold_in(jax.random.fold_in(arg_keys[9], part), 71), part),
        "direction": draw_direction(jax.random.fold_in(jax.random.fold_in(arg_keys[9], part), 71), part),
    }


ROOT_THREE = 1.7320508075688772
MATERN_LENGTH = 0.5
TAPER_CUTOFF = 1.0

def taper_kernel(own_pos, other_pos):
    delta_x = own_pos[0][:, None, None] - other_pos[:, 0][None, :, :]
    delta_y = own_pos[1][:, None, None] - other_pos[:, 1][None, :, :]
    distance = jnp.sqrt(delta_x * delta_x + delta_y * delta_y)
    scaled_dist = distance * (ROOT_THREE / MATERN_LENGTH)
    fraction = jnp.minimum(distance / TAPER_CUTOFF, 1.0)
    return (1.0 + scaled_dist) * jnp.exp(-scaled_dist) * (1.0 - fraction) ** 4 * (1.0 + 4.0 * fraction)

def reference(positions, region_cell, spread, obs_var, counts, pair_flags, iterate, residual, direction):
    region_count = NRR * NRC
    live_mask = (lax.broadcasted_iota(jnp.int32, spread.shape, 2) < counts[:, :, None]).astype(jnp.float32)
    cell_rows = (region_cell // NRC).astype(jnp.float32)
    cell_cols = (region_cell % NRC).astype(jnp.float32)
    corner = jnp.stack([cell_rows, cell_cols], axis=2)[:, :, :, None]
    located = positions + corner
    masked_dir = live_mask * direction
    masked_res = live_mask * residual
    weighted = (spread * masked_dir).reshape(region_count, SLOT)
    flat_pos = located.reshape(region_count, 2, SLOT)
    flag_table = pair_flags.reshape(region_count, region_count)
    partners = jnp.argsort(1 - flag_table, axis=1, stable=True)[:, :NBR].astype(jnp.int32)
    partner_weight = jnp.take_along_axis(flag_table, partners, axis=1).astype(jnp.float32)

    def one_region(packed):
        own_pos, own_sig, pair_picks, weights = packed
        kernel_vals = taper_kernel(own_pos, flat_pos[pair_picks])
        summed = lax.optimization_barrier(jnp.sum(kernel_vals * (weighted[pair_picks] * weights[:, None])[None, :, :], axis=(1, 2)))
        return summed * own_sig
    coupled = lax.map(one_region, (flat_pos, spread.reshape(region_count, SLOT), partners, partner_weight))
    coupled = coupled.reshape(NRR, NRC, SLOT)
    image = live_mask * (coupled + obs_var * masked_dir)
    res_norm = jnp.sum(masked_res * masked_res)
    curvature = jnp.sum(masked_dir * image)
    step_size = res_norm / curvature
    iterate_next = live_mask * iterate + step_size * masked_dir
    residual_next = masked_res - step_size * image
    next_norm = jnp.sum(residual_next * residual_next)
    direction_next = residual_next + next_norm / res_norm * masked_dir
    return (iterate_next, residual_next, direction_next)
```

```python
import functools

import jax
import jax.numpy as jnp
from jax import lax
from jax.experimental import pallas as pl
from jax.experimental.pallas import tpu as pltpu
from jax.sharding import PartitionSpec as P

ROOT_THREE = 1.7320508075688772
MATERN_LENGTH = 0.5
RATE = ROOT_THREE / MATERN_LENGTH
MESH = pl.DeviceIdType.MESH
LANES = 128
CHUNK = 32
VMEM_BYTES = 40 * 1024 * 1024


def remote(src, dst, send_sem, recv_sem, device):
    return pltpu.make_async_remote_copy(
        src_ref=src,
        dst_ref=dst,
        send_sem=send_sem,
        recv_sem=recv_sem,
        device_id=device,
        device_id_type=MESH,
    )


def slot_numbers(shape):
    tile_at = lax.broadcasted_iota(jnp.int32, shape, 1)
    return tile_at * LANES + lax.broadcasted_iota(jnp.int32, shape, 2)


def gather_kernel(
    row_count, col_count, pos_ref, cell_ref, count_ref, spread_ref, dir_ref,
    row_out, row_meta, col_out, col_meta, send_row, recv_row, send_col, recv_col,
):
    my_row, my_col = lax.axis_index("rows"), lax.axis_index("cols")
    row_peers = [lax.rem(my_row + step, row_count) for step in range(1, row_count)]
    col_peers = [lax.rem(my_col + step, col_count) for step in range(1, col_count)]

    barrier = pltpu.get_barrier_semaphore()
    for peer in row_peers:
        pl.semaphore_signal(barrier, inc=1, device_id={"rows": peer}, device_id_type=MESH)
    for peer in col_peers:
        pl.semaphore_signal(barrier, inc=1, device_id={"cols": peer}, device_id_type=MESH)

    local_rows, tiles, _ = spread_ref.shape
    cell = cell_ref[...].astype(jnp.float32)
    counts = count_ref[...]
    cell_row = jnp.floor((cell + 0.5) * (1.0 / col_count))
    cell_col = cell - cell_row * col_count
    live = slot_numbers((local_rows, tiles, LANES)) < counts.reshape(local_rows, 1, 1)
    weighted = spread_ref[...] * jnp.where(live, dir_ref[...], 0.0)
    lane_at = lax.broadcasted_iota(jnp.int32, (local_rows, LANES), 1)
    meta = jnp.where(
        lane_at == 0,
        counts,
        jnp.where(lane_at == 1, cell_row.astype(jnp.int32), cell_col.astype(jnp.int32)),
    )
    for axis, corner in enumerate((cell_row, cell_col)):
        for tile in range(tiles):
            line = pos_ref[:, axis, tile * LANES : (tile + 1) * LANES] + corner
            row_out[my_col, axis, :, tile, :] = line
            col_out[my_row, axis, :, tile, :] = line
    row_out[my_col, 2] = weighted
    col_out[my_row, 2] = weighted
    row_meta[my_col] = meta
    col_meta[my_row] = meta

    pl.semaphore_wait(barrier, row_count + col_count - 2)
    copies = []
    for peer in row_peers:
        for kind, ref in enumerate((col_out, col_meta)):
            copies.append((ref, my_row, peer, send_row.at[kind], recv_row.at[kind], "rows"))
    for peer in col_peers:
        for kind, ref in enumerate((row_out, row_meta)):
            copies.append((ref, my_col, peer, send_col.at[kind], recv_col.at[kind], "cols"))
    for ref, mine, peer, sends, recvs, axis in copies:
        remote(ref.at[mine], ref.at[mine], sends.at[peer], recvs.at[mine], {axis: peer}).start()
    for ref, mine, peer, sends, recvs, axis in copies:
        landed = remote(ref.at[mine], ref.at[peer], sends.at[peer], recvs.at[peer], {axis: peer})
        landed.wait_send()
        landed.wait_recv()


def covariance(delta_x, delta_y):
    square = jnp.maximum(delta_x * delta_x + delta_y * delta_y, 1e-30)
    square = jnp.minimum(square, 1.0)
    distance = square * lax.rsqrt(square)
    gap = 1.0 - distance
    gap = gap * gap
    gap = gap * gap
    growth = (4.0 * RATE * distance + (4.0 + RATE)) * distance + 1.0
    return growth * gap * jnp.exp(distance * (-RATE))


def pair_kernel(
    row_meta, col_meta, row_ref, col_ref, row_sum, col_sum, own_x, own_y, own_w, own_acc, other_acc
):
    col_count, _, local_rows, _, _ = row_ref.shape
    row_count = col_ref.shape[0]
    my_row, my_col = lax.axis_index("rows"), lax.axis_index("cols")
    row_sum[...] = jnp.zeros_like(row_sum)
    col_sum[...] = jnp.zeros_like(col_sum)

    def spread_out(line):
        return jnp.broadcast_to(line, (LANES, LANES)).T

    def one_pair(own_group, own_line, other_group, other_line, own_count, other_count, same):
        own_tiles = (own_count + LANES - 1) // LANES
        other_tiles = (other_count + LANES - 1) // LANES

        def clear(tile, carry):
            other_acc[tile] = jnp.zeros((8, LANES), jnp.float32)
            return carry

        lax.fori_loop(0, other_tiles, clear, 0)
        keep = jnp.where(same, 0.0, 1.0)

        def own_tile(tile, carry):
            here = pl.ds(tile, 1)
            own_x[...] = spread_out(row_ref[own_group, 0, own_line, here, :])
            own_y[...] = spread_out(row_ref[own_group, 1, own_line, here, :])
            own_w[...] = spread_out(row_ref[own_group, 2, own_line, here, :] * keep)
            own_acc[...] = jnp.zeros_like(own_acc)

            def body(first, width):
                lines = []
                for step in range(width):
                    there = pl.ds(first + step, 1)
                    lines.append(
                        [col_ref[other_group, plane, other_line, there, :] for plane in range(3)]
                    )
                totals = [other_acc[first + step] for step in range(width)]
                for start in range(0, LANES, CHUNK):
                    part = pl.ds(start, CHUNK)
                    part_x, part_y, part_w = own_x[part, :], own_y[part, :], own_w[part, :]
                    part_acc = own_acc[part, :]
                    for step in range(width):
                        line_x, line_y, line_w = lines[step]
                        value = covariance(part_x - line_x, part_y - line_y)
                        part_acc = part_acc + value * line_w
                        backward = value * part_w
                        totals[step] = totals[step] + jnp.sum(
                            backward.reshape(CHUNK // 8, 8, LANES), axis=0
                        )
                    own_acc[part, :] = part_acc
                for step in range(width):
                    other_acc[first + step] = totals[step]

            def two(index, inner):
                body(index * 2, 2)
                return inner

            lax.fori_loop(0, other_tiles // 2, two, 0)

            @pl.when(other_tiles % 2 == 1)
            def _():
                body(other_tiles - 1, 1)

            row_sum[own_group, own_line, here, :] += jnp.sum(
                own_acc[...].T, axis=0, keepdims=True
            )
            return carry

        lax.fori_loop(0, own_tiles, own_tile, 0)

        def finish(tile, carry):
            col_sum[other_group, other_line, pl.ds(tile, 1), :] += jnp.sum(
                other_acc[tile], axis=0, keepdims=True
            )
            return carry

        lax.fori_loop(0, other_tiles, finish, 0)

    def own_region(own, carry):
        own_group, own_line = own // local_rows, own % local_rows
        own_count = row_meta[own_group, own_line, 0]
        own_cell_row = row_meta[own_group, own_line, 1]
        own_cell_col = row_meta[own_group, own_line, 2]
        own_id = (my_row * local_rows + own_line) * col_count + own_group

        def other_region(other, inner):
            other_group, other_line = other // local_rows, other % local_rows
            other_id = other * col_count + my_col
            near = (jnp.abs(col_meta[other_group, other_line, 1] - own_cell_row) <= 1) & (
                jnp.abs(col_meta[other_group, other_line, 2] - own_cell_col) <= 1
            )
            odd = (own_id + other_id) % 2 == 1
            mine = (own_id == other_id) | (odd == (own_id < other_id))

            @pl.when(near & mine)
            def _():
                one_pair(
                    own_group,
                    own_line,
                    other_group,
                    other_line,
                    own_count,
                    col_meta[other_group, other_line, 0],
                    own_id == other_id,
                )

            return inner

        return lax.fori_loop(0, row_count * local_rows, other_region, carry)

    lax.fori_loop(0, col_count * local_rows, own_region, 0)


def step_kernel(
    row_count, col_count, row_sum, col_sum, spread_ref, var_ref, dir_ref, res_ref, iter_ref,
    count_ref, iter_out, res_out, dir_out, row_land, col_land, stats, mine_stats,
    send_row, recv_row, send_col, recv_col, send_stat, recv_stat,
):
    my_row, my_col = lax.axis_index("rows"), lax.axis_index("cols")
    device_count = row_count * col_count
    me = my_row * col_count + my_col
    row_peers = [lax.rem(my_row + step, row_count) for step in range(1, row_count)]
    col_peers = [lax.rem(my_col + step, col_count) for step in range(1, col_count)]

    def place(peer):
        return {"rows": peer // col_count, "cols": peer % col_count}

    barrier = pltpu.get_barrier_semaphore()

    def greet(step, carry):
        peer = lax.rem(me + step, device_count)
        pl.semaphore_signal(barrier, inc=1, device_id=place(peer), device_id_type=MESH)
        return carry

    lax.fori_loop(1, device_count, greet, 0)
    live = slot_numbers(spread_ref.shape) < count_ref[...]
    masked_dir = jnp.where(live, dir_ref[...], 0.0)
    masked_res = jnp.where(live, res_ref[...], 0.0)
    pl.semaphore_wait(barrier, device_count - 1)

    copies = []
    for peer in row_peers:
        copies.append((col_sum, col_land, my_row, peer, send_row, recv_row, "rows"))
    for peer in col_peers:
        copies.append((row_sum, row_land, my_col, peer, send_col, recv_col, "cols"))
    for src, dst, mine, peer, sends, recvs, axis in copies:
        remote(src.at[peer], dst.at[mine], sends.at[peer], recvs.at[mine], {axis: peer}).start()
    total = row_sum[my_col] + col_sum[my_row]
    for src, dst, mine, peer, sends, recvs, axis in copies:
        landed = remote(src.at[peer], dst.at[peer], sends.at[peer], recvs.at[peer], {axis: peer})
        landed.wait_send()
        landed.wait_recv()
        total = total + dst[peer]

    image = jnp.where(live, spread_ref[...] * total + var_ref[...] * masked_dir, 0.0)

    def lane_sum(values):
        return jnp.sum(jnp.sum(values, axis=0), axis=0, keepdims=True)

    for index, values in enumerate(
        (masked_res * masked_res, masked_dir * image, masked_res * image, image * image)
    ):
        mine_stats[pl.ds(index, 1), :] = lane_sum(values)
    stats[me] = mine_stats[...]

    def send_stats(step, carry):
        peer = lax.rem(me + step, device_count)
        remote(
            mine_stats, stats.at[me], send_stat.at[peer], recv_stat.at[me], place(peer)
        ).start()
        return carry

    def wait_stats(step, carry):
        peer = lax.rem(me + step, device_count)
        landed = remote(
            mine_stats, stats.at[peer], send_stat.at[peer], recv_stat.at[peer], place(peer)
        )
        landed.wait_send()
        landed.wait_recv()
        return carry

    lax.fori_loop(1, device_count, send_stats, 0)
    lax.fori_loop(1, device_count, wait_stats, 0)
    sums = jnp.sum(jnp.sum(stats[...], axis=0), axis=1, keepdims=True)
    res_norm, curvature, cross, image_norm = (sums[at : at + 1, :][None] for at in range(4))
    step_size = res_norm / curvature
    next_norm = res_norm - 2.0 * step_size * cross + step_size * step_size * image_norm
    residual_next = masked_res - step_size * image
    iter_out[...] = jnp.where(live, iter_ref[...], 0.0) + step_size * masked_dir
    res_out[...] = residual_next
    dir_out[...] = residual_next + next_norm / res_norm * masked_dir


def vmem(count):
    return [pl.BlockSpec(memory_space=pltpu.VMEM)] * count


def local(
    row_count, col_count, positions, region_cell, spread, obs_var, counts, pair_flags, iterate,
    residual, direction,
):
    local_rows, _, slots = spread.shape
    tiles = slots // LANES
    flat = (local_rows, tiles, LANES)
    device_count = row_count * col_count
    f32, i32 = jnp.float32, jnp.int32
    dma = pltpu.SemaphoreType.DMA
    spread_l, var_l, iter_l, res_l, dir_l = (
        value.reshape(flat) for value in (spread, obs_var, iterate, residual, direction)
    )
    row_part, row_meta, col_part, col_meta = pl.pallas_call(
        functools.partial(gather_kernel, row_count, col_count),
        out_shape=(
            jax.ShapeDtypeStruct((col_count, 3, local_rows, tiles, LANES), f32),
            jax.ShapeDtypeStruct((col_count, local_rows, LANES), i32),
            jax.ShapeDtypeStruct((row_count, 3, local_rows, tiles, LANES), f32),
            jax.ShapeDtypeStruct((row_count, local_rows, LANES), i32),
        ),
        in_specs=vmem(5),
        out_specs=tuple(vmem(4)),
        scratch_shapes=[
            dma((2, row_count)),
            dma((2, row_count)),
            dma((2, col_count)),
            dma((2, col_count)),
        ],
        compiler_params=pltpu.CompilerParams(
            collective_id=0, has_side_effects=True, vmem_limit_bytes=VMEM_BYTES
        ),
        name="gather_parts",
    )(positions.reshape(local_rows, 2, slots), region_cell, counts, spread_l, dir_l)

    row_sum, col_sum = pl.pallas_call(
        pair_kernel,
        out_shape=(
            jax.ShapeDtypeStruct((col_count, local_rows, tiles, LANES), f32),
            jax.ShapeDtypeStruct((row_count, local_rows, tiles, LANES), f32),
        ),
        in_specs=[pl.BlockSpec(memory_space=pltpu.SMEM)] * 2 + vmem(2),
        out_specs=tuple(vmem(2)),
        scratch_shapes=[pltpu.VMEM((LANES, LANES), f32)] * 4
        + [pltpu.VMEM((tiles, 8, LANES), f32)],
        compiler_params=pltpu.CompilerParams(vmem_limit_bytes=VMEM_BYTES),
        name="pair_sums",
    )(row_meta, col_meta, row_part, col_part)

    outs = pl.pallas_call(
        functools.partial(step_kernel, row_count, col_count),
        out_shape=(jax.ShapeDtypeStruct(flat, f32),) * 3,
        in_specs=vmem(8),
        out_specs=tuple(vmem(3)),
        scratch_shapes=[
            pltpu.VMEM((col_count, local_rows, tiles, LANES), f32),
            pltpu.VMEM((row_count, local_rows, tiles, LANES), f32),
            pltpu.VMEM((device_count, 4, LANES), f32),
            pltpu.VMEM((4, LANES), f32),
            dma((row_count,)),
            dma((row_count,)),
            dma((col_count,)),
            dma((col_count,)),
            dma((device_count,)),
            dma((device_count,)),
        ],
        compiler_params=pltpu.CompilerParams(
            collective_id=1, has_side_effects=True, vmem_limit_bytes=VMEM_BYTES
        ),
        name="reduce_and_step",
    )(row_sum, col_sum, spread_l, var_l, dir_l, res_l, iter_l, counts.reshape(local_rows, 1, 1))
    return tuple(out.reshape(spread.shape) for out in outs)


def solution(mesh):
    per_slot = P(("groups", "rows"), "cols", None)
    return jax.shard_map(
        functools.partial(local, mesh.shape["rows"], mesh.shape["cols"]),
        mesh=mesh,
        in_specs=(
            P(("groups", "rows"), "cols", None, None),
            P(("groups", "rows"), "cols"),
            per_slot,
            per_slot,
            P(("groups", "rows"), "cols"),
            P(("groups", "rows"), None, None, "cols"),
            per_slot,
            per_slot,
            per_slot,
        ),
        out_specs=(per_slot, per_slot, per_slot),
        check_vma=False,
    )
```

```python
import functools
import math

import jax
import jax.numpy as jnp
from jax import lax
from jax.experimental import pallas as pl
from jax.experimental.pallas import tpu as pltpu
from jax.sharding import PartitionSpec as P

ROOT_THREE = 1.7320508075688772
MATERN_LENGTH = 0.5
RATE = ROOT_THREE / MATERN_LENGTH
MESH = pl.DeviceIdType.MESH
LANES = 128
CHUNK = 32
BITS = RATE / math.log(2.0)
SCALE = 4.0 * RATE * BITS**-6 * 2.0**-BITS
TILE_COST, OWN_COST, PAIR_COST = 100, 130, 150
VMEM_BYTES = 40 * 1024 * 1024


def remote(src, dst, send_sem, recv_sem, device):
    return pltpu.make_async_remote_copy(
        src_ref=src,
        dst_ref=dst,
        send_sem=send_sem,
        recv_sem=recv_sem,
        device_id=device,
        device_id_type=MESH,
    )


def slot_numbers(shape):
    tile_at = lax.broadcasted_iota(jnp.int32, shape, 1)
    return tile_at * LANES + lax.broadcasted_iota(jnp.int32, shape, 2)


def gather_kernel(
    row_count, col_count, pos_ref, cell_ref, count_ref, spread_ref, dir_ref,
    row_out, col_out, meta_out, send_row, recv_row, send_col, recv_col, send_meta, recv_meta,
):
    my_row, my_col = lax.axis_index("rows"), lax.axis_index("cols")
    row_peers = [lax.rem(my_row + step, row_count) for step in range(1, row_count)]
    col_peers = [lax.rem(my_col + step, col_count) for step in range(1, col_count)]

    device_count = row_count * col_count
    me = my_row * col_count + my_col

    def place(peer):
        return {"rows": peer // col_count, "cols": peer % col_count}

    barrier = pltpu.get_barrier_semaphore()

    def greet(step, carry):
        peer = lax.rem(me + step, device_count)
        pl.semaphore_signal(barrier, inc=1, device_id=place(peer), device_id_type=MESH)
        return carry

    lax.fori_loop(1, device_count, greet, 0)
    local_rows, tiles, _ = spread_ref.shape
    cell = cell_ref[...].astype(jnp.float32)
    counts = count_ref[...]
    cell_row = jnp.floor((cell + 0.5) * (1.0 / col_count))
    cell_col = cell - cell_row * col_count
    live = slot_numbers((local_rows, tiles, LANES)) < counts.reshape(local_rows, 1, 1)
    weighted = spread_ref[...] * jnp.where(live, dir_ref[...], 0.0)
    line_at = lax.broadcasted_iota(jnp.int32, (local_rows, LANES), 0)
    lane_at = lax.broadcasted_iota(jnp.int32, (local_rows, LANES), 1)
    meta = jnp.where(
        lane_at == 2 * line_at,
        counts.astype(jnp.float32),
        jnp.where(lane_at == 2 * line_at + 1, cell, 0.0),
    )
    meta_out[me] = jnp.sum(meta, axis=0, keepdims=True).astype(jnp.int32)
    for axis, corner in enumerate((cell_row, cell_col)):
        for tile in range(tiles):
            line = pos_ref[:, axis, tile * LANES : (tile + 1) * LANES] + corner
            row_out[my_col, axis, :, tile, :] = line
            col_out[my_row, axis, :, tile, :] = line
    row_out[my_col, 2] = weighted
    col_out[my_row, 2] = weighted

    pl.semaphore_wait(barrier, device_count - 1)

    def send_metas(step, carry):
        peer = lax.rem(me + step, device_count)
        remote(
            meta_out.at[me], meta_out.at[me], send_meta.at[peer], recv_meta.at[me], place(peer)
        ).start()
        return carry

    def wait_metas(step, carry):
        peer = lax.rem(me + step, device_count)
        landed = remote(
            meta_out.at[me], meta_out.at[peer], send_meta.at[peer], recv_meta.at[peer], place(peer)
        )
        landed.wait_send()
        landed.wait_recv()
        return carry

    copies = []
    for peer in row_peers:
        copies.append((col_out, my_row, peer, send_row, recv_row, "rows"))
    for peer in col_peers:
        copies.append((row_out, my_col, peer, send_col, recv_col, "cols"))
    for ref, mine, peer, sends, recvs, axis in copies:
        remote(ref.at[mine], ref.at[mine], sends.at[peer], recvs.at[mine], {axis: peer}).start()
    lax.fori_loop(1, device_count, send_metas, 0)
    lax.fori_loop(1, device_count, wait_metas, 0)
    for ref, mine, peer, sends, recvs, axis in copies:
        landed = remote(ref.at[mine], ref.at[peer], sends.at[peer], recvs.at[peer], {axis: peer})
        landed.wait_send()
        landed.wait_recv()


def covariance(delta_x, delta_y):
    square = jnp.maximum(delta_x * delta_x + delta_y * delta_y, 1e-30)
    scaled = square * lax.rsqrt(square)
    gap = jnp.maximum(BITS - scaled, 0.0)
    power = jnp.exp2(gap)
    gap = gap * gap
    gap = gap * gap
    growth = (scaled + BITS / 4.0) * (scaled + BITS / RATE)
    return growth * gap * power


def tile_count(slots):
    return lax.shift_right_logical(slots + (LANES - 1), LANES.bit_length() - 1)


def choose_pairs(meta, cell_tiles, cell_row, cell_col, cell_line, load, chosen, sizes):
    row_count, col_count, local_rows = sizes
    grid_rows = row_count * local_rows
    my_row, my_col = lax.axis_index("rows"), lax.axis_index("cols")
    me = my_row * col_count + my_col

    def place_regions(row, carry):
        for col in range(col_count):
            device = row * col_count + col
            load[device] = 0
            for line in range(local_rows):
                cell = meta[device, 2 * line + 1]
                cell_tiles[cell] = tile_count(meta[device, 2 * line])
                cell_row[cell] = row
                cell_col[cell] = col
                cell_line[cell] = line
        return carry

    lax.fori_loop(0, row_count, place_regions, 0)
    for col in range(col_count):
        past = grid_rows * col_count + col
        cell_tiles[past] = 0
        cell_row[past] = 0
        cell_col[past] = 0
        cell_line[past] = 0

    def take(total, device, own_cell, other_cell, present):
        chosen[0, total] = own_cell
        chosen[1, total] = other_cell
        return total + jnp.where((device == me) & present, 1, 0)

    def cost(own_tiles, other_tiles):
        return own_tiles * (TILE_COST * other_tiles + OWN_COST) + PAIR_COST

    def same_cells(row, total):
        for col in range(col_count):
            cell = row * col_count + col
            tiles = cell_tiles[cell]
            device = cell_row[cell] * col_count + cell_col[cell]
            load[device] = load[device] + cost(tiles, tiles)
            total = take(total, device, cell, cell, True)
        return total

    def near_cells(row, total):
        for col in range(col_count):
            first = row * col_count + col
            first_tiles, first_row, first_col = cell_tiles[first], cell_row[first], cell_col[first]
            for down, across in ((0, 1), (1, -1), (1, 0), (1, 1)):
                if not 0 <= col + across < col_count:
                    continue
                second = first + down * col_count + across
                second_tiles = cell_tiles[second]
                second_row, second_col = cell_row[second], cell_col[second]
                forward = first_row * col_count + second_col
                backward = second_row * col_count + first_col
                forward_load = load[forward] + cost(first_tiles, second_tiles)
                backward_load = load[backward] + cost(second_tiles, first_tiles)
                ahead = forward_load <= backward_load
                present = second_tiles > 0
                device = jnp.where(ahead, forward, backward)
                load[device] = jnp.where(
                    present, jnp.where(ahead, forward_load, backward_load), load[device]
                )
                total = take(
                    total,
                    device,
                    jnp.where(ahead, first, second),
                    jnp.where(ahead, second, first),
                    present,
                )
        return total

    total = lax.fori_loop(0, grid_rows, same_cells, 0)
    return lax.fori_loop(0, grid_rows, near_cells, total)


def pair_kernel(
    meta, row_ref, col_ref, row_sum, col_sum, own_x, own_y, own_w, own_acc, other_acc,
    own_local, other_local, cell_tiles, cell_row, cell_col, cell_line, load, chosen,
):
    col_count, _, local_rows, _, _ = row_ref.shape
    row_count = col_ref.shape[0]
    row_sum[...] = jnp.zeros_like(row_sum)
    col_sum[...] = jnp.zeros_like(col_sum)
    total = choose_pairs(
        meta, cell_tiles, cell_row, cell_col, cell_line, load, chosen,
        (row_count, col_count, local_rows),
    )

    def skewed(line):
        wide = jnp.broadcast_to(line, (LANES, LANES))
        return pltpu.roll(wide, 0, 1, stride=1, stride_axis=0)

    def unskewed_sum(block):
        total = block[0:8]
        for start in range(8, LANES, 8):
            total = total + pltpu.roll(block[start : start + 8], LANES - start, 1)
        line_at = lax.broadcasted_iota(jnp.int32, (8, LANES), 0)
        for bit in (1, 2, 4):
            total = jnp.where((line_at & bit) != 0, pltpu.roll(total, LANES - bit, 1), total)
        return jnp.sum(total, axis=0, keepdims=True)

    def one_pair(index, carry):
        own_cell, other_cell = chosen[0, index], chosen[1, index]
        own_group, own_line = cell_col[own_cell], cell_line[own_cell]
        other_group, other_line = cell_row[other_cell], cell_line[other_cell]
        own_tiles, other_tiles = cell_tiles[own_cell], cell_tiles[other_cell]
        keep = jnp.where(own_cell == other_cell, 0.0, SCALE)
        for axis in range(2):
            origin = row_ref[own_group, axis, own_line, 0:1, 0:1]
            own_local[axis] = (row_ref[own_group, axis, own_line] - origin) * BITS
            other_local[axis] = (col_ref[other_group, axis, other_line] - origin) * BITS
        own_local[2] = row_ref[own_group, 2, own_line] * keep
        other_local[2] = col_ref[other_group, 2, other_line] * SCALE
        other_acc[...] = jnp.zeros_like(other_acc)

        def own_tile(tile, inner):
            here = pl.ds(tile, 1)
            own_x[...] = skewed(own_local[0, here, :])
            own_y[...] = skewed(own_local[1, here, :])
            own_w[...] = skewed(own_local[2, here, :])
            own_acc[...] = jnp.zeros_like(own_acc)

            def body(first, width):
                lines = [
                    [other_local[plane, pl.ds(first + step, 1), :] for plane in range(3)]
                    for step in range(width)
                ]
                totals = [other_acc[first + step] for step in range(width)]
                for start in range(0, LANES, CHUNK):
                    part = pl.ds(start, CHUNK)
                    part_x, part_y, part_w = own_x[part, :], own_y[part, :], own_w[part, :]
                    part_acc = own_acc[part, :]
                    for step in range(width):
                        line_x, line_y, line_w = lines[step]
                        value = covariance(part_x - line_x, part_y - line_y)
                        part_acc = part_acc + value * line_w
                        backward = value * part_w
                        totals[step] = totals[step] + jnp.sum(
                            backward.reshape(CHUNK // 8, 8, LANES), axis=0
                        )
                    own_acc[part, :] = part_acc
                for step in range(width):
                    other_acc[first + step] = totals[step]

            def two(pair, nested):
                body(pair * 2, 2)
                return nested

            lax.fori_loop(0, lax.shift_right_logical(other_tiles, 1), two, 0)

            @pl.when((other_tiles & 1) == 1)
            def _():
                body(other_tiles - 1, 1)

            row_sum[own_group, own_line, here, :] += unskewed_sum(own_acc[...])
            return inner

        lax.fori_loop(0, own_tiles, own_tile, 0)

        def finish(tile, inner):
            col_sum[other_group, other_line, pl.ds(tile, 1), :] += jnp.sum(
                other_acc[tile], axis=0, keepdims=True
            )
            return inner

        lax.fori_loop(0, other_tiles, finish, 0)
        return carry

    lax.fori_loop(0, total, one_pair, 0)


def step_kernel(
    row_count, col_count, row_sum, col_sum, spread_ref, var_ref, dir_ref, res_ref, iter_ref,
    count_ref, iter_out, res_out, dir_out, row_land, col_land, stats, mine_stats,
    send_row, recv_row, send_col, recv_col, send_stat, recv_stat,
):
    my_row, my_col = lax.axis_index("rows"), lax.axis_index("cols")
    device_count = row_count * col_count
    me = my_row * col_count + my_col
    row_peers = [lax.rem(my_row + step, row_count) for step in range(1, row_count)]
    col_peers = [lax.rem(my_col + step, col_count) for step in range(1, col_count)]

    def place(peer):
        return {"rows": peer // col_count, "cols": peer % col_count}

    barrier = pltpu.get_barrier_semaphore()

    def greet(step, carry):
        peer = lax.rem(me + step, device_count)
        pl.semaphore_signal(barrier, inc=1, device_id=place(peer), device_id_type=MESH)
        return carry

    lax.fori_loop(1, device_count, greet, 0)
    live = slot_numbers(spread_ref.shape) < count_ref[...]
    masked_dir = jnp.where(live, dir_ref[...], 0.0)
    masked_res = jnp.where(live, res_ref[...], 0.0)
    pl.semaphore_wait(barrier, device_count - 1)

    copies = []
    for peer in row_peers:
        copies.append((col_sum, col_land, my_row, peer, send_row, recv_row, "rows"))
    for peer in col_peers:
        copies.append((row_sum, row_land, my_col, peer, send_col, recv_col, "cols"))
    for src, dst, mine, peer, sends, recvs, axis in copies:
        remote(src.at[peer], dst.at[mine], sends.at[peer], recvs.at[mine], {axis: peer}).start()
    total = row_sum[my_col] + col_sum[my_row]
    for src, dst, mine, peer, sends, recvs, axis in copies:
        landed = remote(src.at[peer], dst.at[peer], sends.at[peer], recvs.at[peer], {axis: peer})
        landed.wait_send()
        landed.wait_recv()
        total = total + dst[peer]

    image = jnp.where(live, spread_ref[...] * total + var_ref[...] * masked_dir, 0.0)

    def lane_sum(values):
        return jnp.sum(jnp.sum(values, axis=0), axis=0, keepdims=True)

    for index, values in enumerate(
        (masked_res * masked_res, masked_dir * image, masked_res * image, image * image)
    ):
        mine_stats[pl.ds(index, 1), :] = lane_sum(values)
    stats[me] = mine_stats[...]

    def send_stats(step, carry):
        peer = lax.rem(me + step, device_count)
        remote(
            mine_stats, stats.at[me], send_stat.at[peer], recv_stat.at[me], place(peer)
        ).start()
        return carry

    def wait_stats(step, carry):
        peer = lax.rem(me + step, device_count)
        landed = remote(
            mine_stats, stats.at[peer], send_stat.at[peer], recv_stat.at[peer], place(peer)
        )
        landed.wait_send()
        landed.wait_recv()
        return carry

    lax.fori_loop(1, device_count, send_stats, 0)
    lax.fori_loop(1, device_count, wait_stats, 0)
    sums = jnp.sum(jnp.sum(stats[...], axis=0), axis=1, keepdims=True)
    res_norm, curvature, cross, image_norm = (sums[at : at + 1, :][None] for at in range(4))
    step_size = res_norm / curvature
    next_norm = res_norm - 2.0 * step_size * cross + step_size * step_size * image_norm
    residual_next = masked_res - step_size * image
    iter_out[...] = jnp.where(live, iter_ref[...], 0.0) + step_size * masked_dir
    res_out[...] = residual_next
    dir_out[...] = residual_next + next_norm / res_norm * masked_dir


def vmem(count):
    return [pl.BlockSpec(memory_space=pltpu.VMEM)] * count


def local(
    row_count, col_count, positions, region_cell, spread, obs_var, counts, pair_flags, iterate,
    residual, direction,
):
    local_rows, _, slots = spread.shape
    tiles = slots // LANES
    flat = (local_rows, tiles, LANES)
    device_count = row_count * col_count
    f32, i32 = jnp.float32, jnp.int32
    dma = pltpu.SemaphoreType.DMA
    spread_l, var_l, iter_l, res_l, dir_l = (
        value.reshape(flat) for value in (spread, obs_var, iterate, residual, direction)
    )
    grid_cells = device_count * local_rows
    row_part, col_part, meta = pl.pallas_call(
        functools.partial(gather_kernel, row_count, col_count),
        out_shape=(
            jax.ShapeDtypeStruct((col_count, 3, local_rows, tiles, LANES), f32),
            jax.ShapeDtypeStruct((row_count, 3, local_rows, tiles, LANES), f32),
            jax.ShapeDtypeStruct((device_count, 1, LANES), i32),
        ),
        in_specs=vmem(5),
        out_specs=tuple(vmem(3)),
        scratch_shapes=[
            dma((row_count,)),
            dma((row_count,)),
            dma((col_count,)),
            dma((col_count,)),
            dma((device_count,)),
            dma((device_count,)),
        ],
        compiler_params=pltpu.CompilerParams(
            collective_id=0, has_side_effects=True, vmem_limit_bytes=VMEM_BYTES
        ),
        name="gather_parts",
    )(positions.reshape(local_rows, 2, slots), region_cell, counts, spread_l, dir_l)

    row_sum, col_sum = pl.pallas_call(
        pair_kernel,
        out_shape=(
            jax.ShapeDtypeStruct((col_count, local_rows, tiles, LANES), f32),
            jax.ShapeDtypeStruct((row_count, local_rows, tiles, LANES), f32),
        ),
        in_specs=[pl.BlockSpec(memory_space=pltpu.SMEM)] + vmem(2),
        out_specs=tuple(vmem(2)),
        scratch_shapes=[pltpu.VMEM((LANES, LANES), f32)] * 4
        + [
            pltpu.VMEM((tiles, 8, LANES), f32),
            pltpu.VMEM((3, tiles, LANES), f32),
            pltpu.VMEM((3, tiles, LANES), f32),
        ]
        + [pltpu.SMEM((grid_cells + col_count,), i32)] * 4
        + [pltpu.SMEM((device_count,), i32), pltpu.SMEM((2, 5 * grid_cells + 1), i32)],
        compiler_params=pltpu.CompilerParams(vmem_limit_bytes=VMEM_BYTES),
        name="pair_sums",
    )(meta.reshape(device_count, LANES), row_part, col_part)

    outs = pl.pallas_call(
        functools.partial(step_kernel, row_count, col_count),
        out_shape=(jax.ShapeDtypeStruct(flat, f32),) * 3,
        in_specs=vmem(8),
        out_specs=tuple(vmem(3)),
        scratch_shapes=[
            pltpu.VMEM((col_count, local_rows, tiles, LANES), f32),
            pltpu.VMEM((row_count, local_rows, tiles, LANES), f32),
            pltpu.VMEM((device_count, 4, LANES), f32),
            pltpu.VMEM((4, LANES), f32),
            dma((row_count,)),
            dma((row_count,)),
            dma((col_count,)),
            dma((col_count,)),
            dma((device_count,)),
            dma((device_count,)),
        ],
        compiler_params=pltpu.CompilerParams(
            collective_id=1, has_side_effects=True, vmem_limit_bytes=VMEM_BYTES
        ),
        name="reduce_and_step",
    )(row_sum, col_sum, spread_l, var_l, dir_l, res_l, iter_l, counts.reshape(local_rows, 1, 1))
    return tuple(out.reshape(spread.shape) for out in outs)


def solution(mesh):
    per_slot = P(("groups", "rows"), "cols", None)
    return jax.shard_map(
        functools.partial(local, mesh.shape["rows"], mesh.shape["cols"]),
        mesh=mesh,
        in_specs=(
            P(("groups", "rows"), "cols", None, None),
            P(("groups", "rows"), "cols"),
            per_slot,
            per_slot,
            P(("groups", "rows"), "cols"),
            P(("groups", "rows"), None, None, "cols"),
            per_slot,
            per_slot,
            per_slot,
        ),
        out_specs=(per_slot, per_slot, per_slot),
        check_vma=False,
    )
```

```python
import functools
import math

import jax
import jax.numpy as jnp
from jax import lax
from jax.experimental import pallas as pl
from jax.experimental.pallas import tpu as pltpu
from jax.sharding import PartitionSpec as P

ROOT_THREE = 1.7320508075688772
MATERN_LENGTH = 0.5
RATE = ROOT_THREE / MATERN_LENGTH
MESH = pl.DeviceIdType.MESH
LANES = 128
CHUNK = 32
GROUP = 2
BITS = RATE / math.log(2.0)
SCALE = 4.0 * RATE * BITS**-6 * 2.0**-BITS
TILE_COST, OWN_COST, PAIR_COST = 100, 130, 150
VMEM_BYTES = 40 * 1024 * 1024


def remote(src, dst, send_sem, recv_sem, device):
    return pltpu.make_async_remote_copy(
        src_ref=src,
        dst_ref=dst,
        send_sem=send_sem,
        recv_sem=recv_sem,
        device_id=device,
        device_id_type=MESH,
    )


def slot_numbers(shape):
    tile_at = lax.broadcasted_iota(jnp.int32, shape, 1)
    return tile_at * LANES + lax.broadcasted_iota(jnp.int32, shape, 2)


def gather_kernel(
    row_count, col_count, pos_ref, cell_ref, count_ref, spread_ref, dir_ref,
    row_out, col_out, meta_out, send_row, recv_row, send_col, recv_col, send_meta, recv_meta,
):
    my_row, my_col = lax.axis_index("rows"), lax.axis_index("cols")
    row_peers = [lax.rem(my_row + step, row_count) for step in range(1, row_count)]
    col_peers = [lax.rem(my_col + step, col_count) for step in range(1, col_count)]

    device_count = row_count * col_count
    me = my_row * col_count + my_col

    def place(peer):
        return {"rows": peer // col_count, "cols": peer % col_count}

    barrier = pltpu.get_barrier_semaphore()

    def greet(step, carry):
        peer = lax.rem(me + step, device_count)
        pl.semaphore_signal(barrier, inc=1, device_id=place(peer), device_id_type=MESH)
        return carry

    lax.fori_loop(1, device_count, greet, 0)
    local_rows, tiles, _ = spread_ref.shape
    cell = cell_ref[...].astype(jnp.float32)
    counts = count_ref[...]
    cell_row = jnp.floor((cell + 0.5) * (1.0 / col_count))
    cell_col = cell - cell_row * col_count
    live = slot_numbers((local_rows, tiles, LANES)) < counts.reshape(local_rows, 1, 1)
    weighted = spread_ref[...] * jnp.where(live, dir_ref[...], 0.0)
    line_at = lax.broadcasted_iota(jnp.int32, (local_rows, LANES), 0)
    lane_at = lax.broadcasted_iota(jnp.int32, (local_rows, LANES), 1)
    meta = jnp.where(
        lane_at == 2 * line_at,
        counts.astype(jnp.float32),
        jnp.where(lane_at == 2 * line_at + 1, cell, 0.0),
    )
    meta_out[me] = jnp.sum(meta, axis=0, keepdims=True).astype(jnp.int32)
    for axis, corner in enumerate((cell_row, cell_col)):
        for tile in range(tiles):
            line = pos_ref[:, axis, tile * LANES : (tile + 1) * LANES] + corner
            row_out[my_col, axis, :, tile, :] = line
            col_out[my_row, axis, :, tile, :] = line
    row_out[my_col, 2] = weighted
    col_out[my_row, 2] = weighted

    pl.semaphore_wait(barrier, device_count - 1)

    def send_metas(step, carry):
        peer = lax.rem(me + step, device_count)
        remote(
            meta_out.at[me], meta_out.at[me], send_meta.at[peer], recv_meta.at[me], place(peer)
        ).start()
        return carry

    def wait_metas(step, carry):
        peer = lax.rem(me + step, device_count)
        landed = remote(
            meta_out.at[me], meta_out.at[peer], send_meta.at[peer], recv_meta.at[peer], place(peer)
        )
        landed.wait_send()
        landed.wait_recv()
        return carry

    copies = []
    for peer in row_peers:
        copies.append((col_out, my_row, peer, send_row, recv_row, "rows"))
    for peer in col_peers:
        copies.append((row_out, my_col, peer, send_col, recv_col, "cols"))
    for ref, mine, peer, sends, recvs, axis in copies:
        remote(ref.at[mine], ref.at[mine], sends.at[peer], recvs.at[mine], {axis: peer}).start()
    lax.fori_loop(1, device_count, send_metas, 0)
    lax.fori_loop(1, device_count, wait_metas, 0)
    for ref, mine, peer, sends, recvs, axis in copies:
        landed = remote(ref.at[mine], ref.at[peer], sends.at[peer], recvs.at[peer], {axis: peer})
        landed.wait_send()
        landed.wait_recv()


def covariance(delta_x, delta_y):
    square = jnp.maximum(delta_x * delta_x + delta_y * delta_y, 1e-30)
    scaled = square * lax.rsqrt(square)
    gap = jnp.maximum(BITS - scaled, 0.0)
    power = jnp.exp2(gap)
    gap = gap * gap
    gap = gap * gap
    growth = (scaled + BITS / 4.0) * (scaled + BITS / RATE)
    return growth * gap * power


def tile_count(slots):
    return lax.shift_right_logical(slots + (LANES - 1), LANES.bit_length() - 1)


def choose_pairs(meta, cell_tiles, cell_row, cell_col, cell_line, load, chosen, sizes):
    row_count, col_count, local_rows = sizes
    grid_rows = row_count * local_rows
    my_row, my_col = lax.axis_index("rows"), lax.axis_index("cols")
    me = my_row * col_count + my_col

    def place_regions(row, carry):
        for col in range(col_count):
            device = row * col_count + col
            load[device] = 0
            for line in range(local_rows):
                cell = meta[device, 2 * line + 1]
                cell_tiles[cell] = tile_count(meta[device, 2 * line])
                cell_row[cell] = row
                cell_col[cell] = col
                cell_line[cell] = line
        return carry

    lax.fori_loop(0, row_count, place_regions, 0)
    for col in range(col_count):
        past = grid_rows * col_count + col
        cell_tiles[past] = 0
        cell_row[past] = 0
        cell_col[past] = 0
        cell_line[past] = 0

    def take(total, device, own_cell, other_cell, present):
        chosen[0, total] = own_cell
        chosen[1, total] = other_cell
        return total + jnp.where((device == me) & present, 1, 0)

    def cost(own_tiles, other_tiles):
        least = jnp.minimum(own_tiles, other_tiles)
        return TILE_COST * own_tiles * other_tiles + OWN_COST * least + PAIR_COST

    def same_cells(row, total):
        for col in range(col_count):
            cell = row * col_count + col
            tiles = cell_tiles[cell]
            device = cell_row[cell] * col_count + cell_col[cell]
            load[device] = load[device] + cost(tiles, tiles)
            total = take(total, device, cell, cell, True)
        return total

    def near_cells(row, total):
        for col in range(col_count):
            first = row * col_count + col
            first_tiles, first_row, first_col = cell_tiles[first], cell_row[first], cell_col[first]
            for down, across in ((0, 1), (1, -1), (1, 0), (1, 1)):
                if not 0 <= col + across < col_count:
                    continue
                second = first + down * col_count + across
                second_tiles = cell_tiles[second]
                second_row, second_col = cell_row[second], cell_col[second]
                forward = first_row * col_count + second_col
                backward = second_row * col_count + first_col
                work = cost(first_tiles, second_tiles)
                forward_load, backward_load = load[forward], load[backward]
                ahead = forward_load <= backward_load
                present = second_tiles > 0
                device = jnp.where(ahead, forward, backward)
                load[device] = jnp.minimum(forward_load, backward_load) + jnp.where(
                    present, work, 0
                )
                total = take(
                    total,
                    device,
                    jnp.where(ahead, first, second),
                    jnp.where(ahead, second, first),
                    present,
                )
        return total

    total = lax.fori_loop(0, grid_rows, same_cells, 0)
    return lax.fori_loop(0, grid_rows, near_cells, total)


def pair_kernel(
    meta, row_ref, col_ref, row_sum, col_sum, own_wide, own_acc, other_acc,
    own_local, other_local, sums, cell_tiles, cell_row, cell_col, cell_line, load, chosen,
):
    col_count, _, local_rows, _, _ = row_ref.shape
    row_count = col_ref.shape[0]
    row_sum[...] = jnp.zeros_like(row_sum)
    col_sum[...] = jnp.zeros_like(col_sum)
    total = choose_pairs(
        meta, cell_tiles, cell_row, cell_col, cell_line, load, chosen,
        (row_count, col_count, local_rows),
    )

    def one_pair(index, carry):
        row_cell, col_cell = chosen[0, index], chosen[1, index]
        row_group, row_line = cell_col[row_cell], cell_line[row_cell]
        col_group, col_line = cell_row[col_cell], cell_line[col_cell]
        row_tiles, col_tiles = cell_tiles[row_cell], cell_tiles[col_cell]
        swap = col_tiles < row_tiles
        own_tiles = jnp.minimum(row_tiles, col_tiles)
        other_tiles = jnp.maximum(row_tiles, col_tiles)
        keep = jnp.where(row_cell == col_cell, 0.0, SCALE)
        for axis in range(2):
            origin = row_ref[row_group, axis, row_line, 0:1, 0:1]
            row_axis = (row_ref[row_group, axis, row_line] - origin) * BITS
            col_axis = (col_ref[col_group, axis, col_line] - origin) * BITS
            own_local[axis] = jnp.where(swap, col_axis, row_axis)
            other_local[axis] = jnp.where(swap, row_axis, col_axis)
        row_weight = row_ref[row_group, 2, row_line] * keep
        col_weight = col_ref[col_group, 2, col_line] * SCALE
        own_local[2] = jnp.where(swap, col_weight, row_weight)
        other_local[2] = jnp.where(swap, row_weight, col_weight)
        other_acc[...] = jnp.zeros_like(other_acc)
        sums[...] = jnp.zeros_like(sums)

        def spread_out(group, inner):
            for step in range(GROUP):
                tile = group * GROUP + step
                here = pl.ds(tile, 1)
                for plane in range(3):
                    line = jnp.broadcast_to(own_local[plane, here, :], (LANES, LANES))
                    own_wide[tile, plane] = line.T
            return inner

        groups = lax.shift_right_logical(own_tiles + (GROUP - 1), GROUP.bit_length() - 1)
        lax.fori_loop(0, groups, spread_out, 0)

        def own_tile(tile, inner):
            def body(first, width, fresh):
                lines = [
                    [other_local[plane, pl.ds(first + step, 1), :] for plane in range(3)]
                    for step in range(width)
                ]
                totals = [other_acc[first + step] for step in range(width)]
                for start in range(0, LANES, CHUNK):
                    part = pl.ds(start, CHUNK)
                    part_x, part_y, part_w = (own_wide[tile, plane, part, :] for plane in range(3))
                    part_acc = 0.0 if fresh else own_acc[tile, part, :]
                    for step in range(width):
                        line_x, line_y, line_w = lines[step]
                        value = covariance(part_x - line_x, part_y - line_y)
                        part_acc = part_acc + value * line_w
                        backward = value * part_w
                        totals[step] = totals[step] + jnp.sum(
                            backward.reshape(CHUNK // 8, 8, LANES), axis=0
                        )
                    own_acc[tile, part, :] = part_acc
                for step in range(width):
                    other_acc[first + step] = totals[step]

            odd = other_tiles & 1

            @pl.when(odd == 1)
            def _():
                body(0, 1, True)

            @pl.when(odd == 0)
            def _():
                body(0, 2, True)

            def two(pair, nested):
                body(pair * 2 + odd, 2, False)
                return nested

            lax.fori_loop(1 - odd, lax.shift_right_logical(other_tiles, 1), two, 0)
            return inner

        lax.fori_loop(0, own_tiles, own_tile, 0)

        def own_finish(group, inner):
            for step in range(GROUP):
                tile = group * GROUP + step
                sums[0, pl.ds(tile, 1), :] = jnp.sum(own_acc[tile].T, axis=0, keepdims=True)
            return inner

        lax.fori_loop(0, groups, own_finish, 0)

        def other_finish(tile, inner):
            sums[1, pl.ds(tile, 1), :] = jnp.sum(other_acc[tile], axis=0, keepdims=True)
            return inner

        lax.fori_loop(0, other_tiles, other_finish, 0)
        row_sum[row_group, row_line] += jnp.where(swap, sums[1], sums[0])
        col_sum[col_group, col_line] += jnp.where(swap, sums[0], sums[1])
        return carry

    lax.fori_loop(0, total, one_pair, 0)


def step_kernel(
    row_count, col_count, row_sum, col_sum, spread_ref, var_ref, dir_ref, res_ref, iter_ref,
    count_ref, iter_out, res_out, dir_out, row_land, col_land, stats, mine_stats,
    send_row, recv_row, send_col, recv_col, send_stat, recv_stat,
):
    my_row, my_col = lax.axis_index("rows"), lax.axis_index("cols")
    device_count = row_count * col_count
    me = my_row * col_count + my_col
    row_peers = [lax.rem(my_row + step, row_count) for step in range(1, row_count)]
    col_peers = [lax.rem(my_col + step, col_count) for step in range(1, col_count)]

    def place(peer):
        return {"rows": peer // col_count, "cols": peer % col_count}

    barrier = pltpu.get_barrier_semaphore()

    def greet(step, carry):
        peer = lax.rem(me + step, device_count)
        pl.semaphore_signal(barrier, inc=1, device_id=place(peer), device_id_type=MESH)
        return carry

    lax.fori_loop(1, device_count, greet, 0)
    live = slot_numbers(spread_ref.shape) < count_ref[...]
    masked_dir = jnp.where(live, dir_ref[...], 0.0)
    masked_res = jnp.where(live, res_ref[...], 0.0)
    pl.semaphore_wait(barrier, device_count - 1)

    copies = []
    for peer in row_peers:
        copies.append((col_sum, col_land, my_row, peer, send_row, recv_row, "rows"))
    for peer in col_peers:
        copies.append((row_sum, row_land, my_col, peer, send_col, recv_col, "cols"))
    for src, dst, mine, peer, sends, recvs, axis in copies:
        remote(src.at[peer], dst.at[mine], sends.at[peer], recvs.at[mine], {axis: peer}).start()
    total = row_sum[my_col] + col_sum[my_row]
    for src, dst, mine, peer, sends, recvs, axis in copies:
        landed = remote(src.at[peer], dst.at[peer], sends.at[peer], recvs.at[peer], {axis: peer})
        landed.wait_send()
        landed.wait_recv()
        total = total + dst[peer]

    image = jnp.where(live, spread_ref[...] * total + var_ref[...] * masked_dir, 0.0)

    def lane_sum(values):
        return jnp.sum(jnp.sum(values, axis=0), axis=0, keepdims=True)

    for index, values in enumerate(
        (masked_res * masked_res, masked_dir * image, masked_res * image, image * image)
    ):
        mine_stats[pl.ds(index, 1), :] = lane_sum(values)
    stats[me] = mine_stats[...]

    def send_stats(step, carry):
        peer = lax.rem(me + step, device_count)
        remote(
            mine_stats, stats.at[me], send_stat.at[peer], recv_stat.at[me], place(peer)
        ).start()
        return carry

    def wait_stats(step, carry):
        peer = lax.rem(me + step, device_count)
        landed = remote(
            mine_stats, stats.at[peer], send_stat.at[peer], recv_stat.at[peer], place(peer)
        )
        landed.wait_send()
        landed.wait_recv()
        return carry

    lax.fori_loop(1, device_count, send_stats, 0)
    lax.fori_loop(1, device_count, wait_stats, 0)
    sums = jnp.sum(jnp.sum(stats[...], axis=0), axis=1, keepdims=True)
    res_norm, curvature, cross, image_norm = (sums[at : at + 1, :][None] for at in range(4))
    step_size = res_norm / curvature
    next_norm = res_norm - 2.0 * step_size * cross + step_size * step_size * image_norm
    residual_next = masked_res - step_size * image
    iter_out[...] = jnp.where(live, iter_ref[...], 0.0) + step_size * masked_dir
    res_out[...] = residual_next
    dir_out[...] = residual_next + next_norm / res_norm * masked_dir


def vmem(count):
    return [pl.BlockSpec(memory_space=pltpu.VMEM)] * count


def local(
    row_count, col_count, positions, region_cell, spread, obs_var, counts, pair_flags, iterate,
    residual, direction,
):
    local_rows, _, slots = spread.shape
    tiles = slots // LANES
    flat = (local_rows, tiles, LANES)
    device_count = row_count * col_count
    f32, i32 = jnp.float32, jnp.int32
    dma = pltpu.SemaphoreType.DMA
    spread_l, var_l, iter_l, res_l, dir_l = (
        value.reshape(flat) for value in (spread, obs_var, iterate, residual, direction)
    )
    grid_cells = device_count * local_rows
    row_part, col_part, meta = pl.pallas_call(
        functools.partial(gather_kernel, row_count, col_count),
        out_shape=(
            jax.ShapeDtypeStruct((col_count, 3, local_rows, tiles, LANES), f32),
            jax.ShapeDtypeStruct((row_count, 3, local_rows, tiles, LANES), f32),
            jax.ShapeDtypeStruct((device_count, 1, LANES), i32),
        ),
        in_specs=vmem(5),
        out_specs=tuple(vmem(3)),
        scratch_shapes=[
            dma((row_count,)),
            dma((row_count,)),
            dma((col_count,)),
            dma((col_count,)),
            dma((device_count,)),
            dma((device_count,)),
        ],
        compiler_params=pltpu.CompilerParams(
            collective_id=0, has_side_effects=True, vmem_limit_bytes=VMEM_BYTES
        ),
        name="gather_parts",
    )(positions.reshape(local_rows, 2, slots), region_cell, counts, spread_l, dir_l)

    row_sum, col_sum = pl.pallas_call(
        pair_kernel,
        out_shape=(
            jax.ShapeDtypeStruct((col_count, local_rows, tiles, LANES), f32),
            jax.ShapeDtypeStruct((row_count, local_rows, tiles, LANES), f32),
        ),
        in_specs=[pl.BlockSpec(memory_space=pltpu.SMEM)] + vmem(2),
        out_specs=tuple(vmem(2)),
        scratch_shapes=[
            pltpu.VMEM((tiles, 3, LANES, LANES), f32),
            pltpu.VMEM((tiles, LANES, LANES), f32),
            pltpu.VMEM((tiles, 8, LANES), f32),
            pltpu.VMEM((3, tiles, LANES), f32),
            pltpu.VMEM((3, tiles, LANES), f32),
            pltpu.VMEM((2, tiles, LANES), f32),
        ]
        + [pltpu.SMEM((grid_cells + col_count,), i32)] * 4
        + [pltpu.SMEM((device_count,), i32), pltpu.SMEM((2, 5 * grid_cells + 1), i32)],
        compiler_params=pltpu.CompilerParams(vmem_limit_bytes=VMEM_BYTES),
        name="pair_sums",
    )(meta.reshape(device_count, LANES), row_part, col_part)

    outs = pl.pallas_call(
        functools.partial(step_kernel, row_count, col_count),
        out_shape=(jax.ShapeDtypeStruct(flat, f32),) * 3,
        in_specs=vmem(8),
        out_specs=tuple(vmem(3)),
        scratch_shapes=[
            pltpu.VMEM((col_count, local_rows, tiles, LANES), f32),
            pltpu.VMEM((row_count, local_rows, tiles, LANES), f32),
            pltpu.VMEM((device_count, 4, LANES), f32),
            pltpu.VMEM((4, LANES), f32),
            dma((row_count,)),
            dma((row_count,)),
            dma((col_count,)),
            dma((col_count,)),
            dma((device_count,)),
            dma((device_count,)),
        ],
        compiler_params=pltpu.CompilerParams(
            collective_id=1, has_side_effects=True, vmem_limit_bytes=VMEM_BYTES
        ),
        name="reduce_and_step",
    )(row_sum, col_sum, spread_l, var_l, dir_l, res_l, iter_l, counts.reshape(local_rows, 1, 1))
    return tuple(out.reshape(spread.shape) for out in outs)


def solution(mesh):
    per_slot = P(("groups", "rows"), "cols", None)
    return jax.shard_map(
        functools.partial(local, mesh.shape["rows"], mesh.shape["cols"]),
        mesh=mesh,
        in_specs=(
            P(("groups", "rows"), "cols", None, None),
            P(("groups", "rows"), "cols"),
            per_slot,
            per_slot,
            P(("groups", "rows"), "cols"),
            P(("groups", "rows"), None, None, "cols"),
            per_slot,
            per_slot,
            per_slot,
        ),
        out_specs=(per_slot, per_slot, per_slot),
        check_vma=False,
    )
```

```python
import functools
import math

import jax
import jax.numpy as jnp
from jax import lax
from jax.experimental import pallas as pl
from jax.experimental.pallas import tpu as pltpu
from jax.sharding import PartitionSpec as P

ROOT_THREE = 1.7320508075688772
MATERN_LENGTH = 0.5
RATE = ROOT_THREE / MATERN_LENGTH
MESH = pl.DeviceIdType.MESH
LANES = 128
CHUNK = 32
GROUP = 2
BITS = RATE / math.log(2.0)
SCALE = 4.0 * RATE * BITS**-6 * 2.0**-BITS
TILE_COST, OWN_COST, PAIR_COST = 100, 220, 150
FIELD = 1 << 15
VMEM_BYTES = 40 * 1024 * 1024


def remote(src, dst, send_sem, recv_sem, device):
    return pltpu.make_async_remote_copy(
        src_ref=src,
        dst_ref=dst,
        send_sem=send_sem,
        recv_sem=recv_sem,
        device_id=device,
        device_id_type=MESH,
    )


def slot_numbers(shape):
    tile_at = lax.broadcasted_iota(jnp.int32, shape, 1)
    return tile_at * LANES + lax.broadcasted_iota(jnp.int32, shape, 2)


def others(row_count, col_count):
    my_row, my_col = lax.axis_index("rows"), lax.axis_index("cols")
    rows = [lax.rem(my_row + step, row_count) for step in range(row_count)]
    cols = [lax.rem(my_col + step, col_count) for step in range(col_count)]
    return [{"rows": row, "cols": col} for row in rows for col in cols][1:]


def greet_all(peers):
    barrier = pltpu.get_barrier_semaphore()
    for peer in peers:
        pl.semaphore_signal(barrier, inc=1, device_id=peer, device_id_type=MESH)
    return barrier


def gather_kernel(
    row_count, col_count, pos_hbm, cell_hbm, count_hbm, spread_hbm, dir_hbm,
    row_out, col_out, meta_out, pos_ref, cell_ref, count_ref, spread_ref, dir_ref, local_sem,
    send_row, recv_row, send_col, recv_col, send_meta, recv_meta,
):
    my_row, my_col = lax.axis_index("rows"), lax.axis_index("cols")
    row_peers = [lax.rem(my_row + step, row_count) for step in range(1, row_count)]
    col_peers = [lax.rem(my_col + step, col_count) for step in range(1, col_count)]
    device_count = row_count * col_count
    me = my_row * col_count + my_col
    loads = [
        pltpu.make_async_copy(src, dst, local_sem.at[index])
        for index, (src, dst) in enumerate(
            (
                (cell_hbm, cell_ref),
                (count_hbm, count_ref),
                (pos_hbm, pos_ref),
                (spread_hbm, spread_ref),
                (dir_hbm, dir_ref),
            )
        )
    ]
    for load in loads:
        load.start()
    peers = others(row_count, col_count)
    barrier = greet_all(peers)

    local_rows, tiles, _ = spread_ref.shape
    for load in loads:
        load.wait()
    lane_at = lax.broadcasted_iota(jnp.int32, (1, LANES), 1)
    slot_at = slot_numbers((1, tiles, LANES))[0]
    meta = jnp.zeros((1, LANES), jnp.int32)
    for line in range(local_rows):
        count = count_ref[:, line : line + 1]
        cell = cell_ref[:, line : line + 1]
        meta = jnp.where(lane_at == 2 * line, count, meta)
        meta = jnp.where(lane_at == 2 * line + 1, cell, meta)
        cell = cell.astype(jnp.float32)
        cell_row = jnp.floor((cell + 0.5) * (1.0 / col_count))
        cell_col = cell - cell_row * col_count
        weighted = spread_ref[line] * jnp.where(slot_at < count, dir_ref[line], 0.0)
        row_out[my_col, 2, line] = weighted
        col_out[my_row, 2, line] = weighted
        for axis, corner in enumerate((cell_row, cell_col)):
            for tile in range(tiles):
                span = slice(tile * LANES, (tile + 1) * LANES)
                located = pos_ref[line, axis : axis + 1, span] + corner
                row_out[my_col, axis, line, tile : tile + 1, :] = located
                col_out[my_row, axis, line, tile : tile + 1, :] = located
    meta_out[me] = meta
    pl.semaphore_wait(barrier, device_count - 1)

    copies = []
    for peer in row_peers:
        copies.append((col_out, my_row, peer, send_row, recv_row, "rows"))
    for peer in col_peers:
        copies.append((row_out, my_col, peer, send_col, recv_col, "cols"))
    for ref, mine, peer, sends, recvs, axis in copies:
        remote(ref.at[mine], ref.at[mine], sends.at[peer], recvs.at[mine], {axis: peer}).start()
    for peer in peers:
        remote(meta_out.at[me], meta_out.at[me], send_meta, recv_meta, peer).start()
    every = meta_out.at[pl.ds(0, device_count - 1)]
    pltpu.make_async_copy(every, every, send_meta).wait()
    pltpu.make_async_copy(every, every, recv_meta).wait()
    for ref, mine, peer, sends, recvs, axis in copies:
        landed = remote(ref.at[mine], ref.at[peer], sends.at[peer], recvs.at[peer], {axis: peer})
        landed.wait_send()
        landed.wait_recv()


def covariance(delta_x, delta_y):
    square = jnp.maximum(delta_x * delta_x + delta_y * delta_y, 1e-30)
    scaled = square * lax.rsqrt(square)
    gap = jnp.maximum(BITS - scaled, 0.0)
    power = jnp.exp2(gap)
    gap = gap * gap
    gap = gap * gap
    growth = (scaled + BITS / 4.0) * (scaled + BITS / RATE)
    return growth * gap * power


def tile_count(slots):
    return lax.shift_right_logical(slots + (LANES - 1), LANES.bit_length() - 1)


def choose_pairs(meta, cell_tiles, cell_row, cell_col, cell_line, load, chosen, sizes):
    row_count, col_count, local_rows = sizes
    grid_rows = row_count * local_rows
    me = lax.axis_index("rows") * col_count + lax.axis_index("cols")

    def cost(first_tiles, second_tiles):
        least = jnp.minimum(first_tiles, second_tiles)
        return TILE_COST * first_tiles * second_tiles + OWN_COST * least + PAIR_COST

    def place_regions(row, carry):
        for col in range(col_count):
            device = row * col_count + col
            total = 0
            for line in range(local_rows):
                cell = meta[device, 2 * line + 1]
                tiles = tile_count(meta[device, 2 * line])
                cell_tiles[cell] = tiles
                cell_row[cell] = row * col_count
                cell_col[cell] = col
                cell_line[cell] = line
                total = total + cost(tiles, tiles)
            load[device] = total
        return carry

    lax.fori_loop(0, row_count, place_regions, 0)
    for col in range(col_count):
        past = grid_rows * col_count + col
        cell_tiles[past] = 0
        cell_row[past] = 0
        cell_col[past] = 0
        cell_line[past] = 0
    for line in range(local_rows):
        chosen[line] = meta[me, 2 * line + 1] * (FIELD + 1)

    def near_cells(row, total):
        for col in range(col_count):
            first = row * col_count + col
            first_tiles, first_row, first_col = cell_tiles[first], cell_row[first], cell_col[first]
            for down, across in ((0, 1), (1, -1), (1, 0), (1, 1)):
                if not 0 <= col + across < col_count:
                    continue
                second = first + down * col_count + across
                second_tiles = cell_tiles[second]
                present = second_tiles > 0
                forward = first_row + cell_col[second]
                backward = cell_row[second] + first_col
                work = jnp.where(present, cost(first_tiles, second_tiles), 0)
                forward_load, backward_load = load[forward], load[backward]
                ahead = forward_load <= backward_load
                device = jnp.where(ahead, forward, backward)
                load[device] = jnp.minimum(forward_load, backward_load) + work
                chosen[total] = jnp.where(
                    ahead, first * FIELD + second, second * FIELD + first
                )
                total = total + jnp.where((device == me) & present, 1, 0)
        return total

    return lax.fori_loop(0, grid_rows, near_cells, local_rows)


def pair_kernel(
    meta, row_ref, col_ref, row_sum, col_sum, own_wide, own_acc, other_acc,
    own_local, other_local, sums, cell_tiles, cell_row, cell_col, cell_line, load, chosen,
):
    col_count, _, local_rows, _, _ = row_ref.shape
    row_count = col_ref.shape[0]
    row_sum[...] = jnp.zeros_like(row_sum)
    col_sum[...] = jnp.zeros_like(col_sum)
    total = choose_pairs(
        meta, cell_tiles, cell_row, cell_col, cell_line, load, chosen,
        (row_count, col_count, local_rows),
    )

    def one_pair(index, carry):
        row_cell = lax.shift_right_logical(chosen[index], FIELD.bit_length() - 1)
        col_cell = chosen[index] & (FIELD - 1)
        row_group, row_line = cell_col[row_cell], cell_line[row_cell]
        col_group, col_line = lax.div(cell_row[col_cell], col_count), cell_line[col_cell]
        row_tiles, col_tiles = cell_tiles[row_cell], cell_tiles[col_cell]
        swap = col_tiles < row_tiles
        own_tiles = jnp.minimum(row_tiles, col_tiles)
        other_tiles = jnp.maximum(row_tiles, col_tiles)
        keep = jnp.where(row_cell == col_cell, 0.0, SCALE)
        for axis in range(2):
            origin = row_ref[row_group, axis, row_line, 0:1, 0:1]
            row_axis = (row_ref[row_group, axis, row_line] - origin) * BITS
            col_axis = (col_ref[col_group, axis, col_line] - origin) * BITS
            own_local[axis] = jnp.where(swap, col_axis, row_axis)
            other_local[axis] = jnp.where(swap, row_axis, col_axis)
        row_weight = row_ref[row_group, 2, row_line] * keep
        col_weight = col_ref[col_group, 2, col_line] * SCALE
        own_local[2] = jnp.where(swap, col_weight, row_weight)
        other_local[2] = jnp.where(swap, row_weight, col_weight)
        other_acc[...] = jnp.zeros_like(other_acc)
        sums[...] = jnp.zeros_like(sums)

        def spread_out(group, inner):
            for step in range(GROUP):
                tile = group * GROUP + step
                here = pl.ds(tile, 1)
                for plane in range(3):
                    line = jnp.broadcast_to(own_local[plane, here, :], (LANES, LANES))
                    own_wide[tile, plane] = line.T
            return inner

        groups = lax.shift_right_logical(own_tiles + (GROUP - 1), GROUP.bit_length() - 1)
        lax.fori_loop(0, groups, spread_out, 0)

        def own_tile(tile, inner):
            def body(first, width, fresh):
                lines = [
                    [other_local[plane, pl.ds(first + step, 1), :] for plane in range(3)]
                    for step in range(width)
                ]
                totals = [other_acc[first + step] for step in range(width)]
                for start in range(0, LANES, CHUNK):
                    part = pl.ds(start, CHUNK)
                    part_x, part_y, part_w = (own_wide[tile, plane, part, :] for plane in range(3))
                    part_acc = 0.0 if fresh else own_acc[tile, part, :]
                    for step in range(width):
                        line_x, line_y, line_w = lines[step]
                        value = covariance(part_x - line_x, part_y - line_y)
                        part_acc = part_acc + value * line_w
                        backward = value * part_w
                        totals[step] = totals[step] + jnp.sum(
                            backward.reshape(CHUNK // 8, 8, LANES), axis=0
                        )
                    own_acc[tile, part, :] = part_acc
                for step in range(width):
                    other_acc[first + step] = totals[step]

            odd = other_tiles & 1

            @pl.when(odd == 1)
            def _():
                body(0, 1, True)

            @pl.when(odd == 0)
            def _():
                body(0, 2, True)

            def two(pair, nested):
                body(pair * 2 + odd, 2, False)
                return nested

            lax.fori_loop(1 - odd, lax.shift_right_logical(other_tiles, 1), two, 0)
            return inner

        lax.fori_loop(0, own_tiles, own_tile, 0)

        def own_finish(group, inner):
            for step in range(GROUP):
                tile = group * GROUP + step
                sums[0, pl.ds(tile, 1), :] = jnp.sum(own_acc[tile].T, axis=0, keepdims=True)
            return inner

        lax.fori_loop(0, groups, own_finish, 0)

        def other_finish(tile, inner):
            sums[1, pl.ds(tile, 1), :] = jnp.sum(other_acc[tile], axis=0, keepdims=True)
            return inner

        lax.fori_loop(0, other_tiles, other_finish, 0)
        row_sum[row_group, row_line] += jnp.where(swap, sums[1], sums[0])
        col_sum[col_group, col_line] += jnp.where(swap, sums[0], sums[1])
        return carry

    lax.fori_loop(0, total, one_pair, 0)


def step_kernel(
    row_count, col_count, row_sum, col_sum, meta_ref, spread_ref, var_ref, dir_ref, res_ref,
    iter_ref, iter_out, res_out, dir_out, row_land, col_land, stats, mine_stats,
    send_row, recv_row, send_col, recv_col, send_stat, recv_stat,
):
    my_row, my_col = lax.axis_index("rows"), lax.axis_index("cols")
    device_count = row_count * col_count
    me = my_row * col_count + my_col
    row_peers = [lax.rem(my_row + step, row_count) for step in range(1, row_count)]
    col_peers = [lax.rem(my_col + step, col_count) for step in range(1, col_count)]
    peers = others(row_count, col_count)
    barrier = greet_all(peers)
    local_rows = spread_ref.shape[0]
    meta = meta_ref[me]
    line_at = lax.broadcasted_iota(jnp.int32, spread_ref.shape, 0)
    counts = jnp.zeros(spread_ref.shape, jnp.int32)
    for line in range(local_rows):
        counts = jnp.where(line_at == line, meta[:, 2 * line : 2 * line + 1][None], counts)
    live = slot_numbers(spread_ref.shape) < counts
    masked_dir = jnp.where(live, dir_ref[...], 0.0)
    masked_res = jnp.where(live, res_ref[...], 0.0)
    pl.semaphore_wait(barrier, device_count - 1)

    copies = []
    for peer in row_peers:
        copies.append((col_sum, col_land, my_row, peer, send_row, recv_row, "rows"))
    for peer in col_peers:
        copies.append((row_sum, row_land, my_col, peer, send_col, recv_col, "cols"))
    for src, dst, mine, peer, sends, recvs, axis in copies:
        remote(src.at[peer], dst.at[mine], sends.at[peer], recvs.at[mine], {axis: peer}).start()
    total = row_sum[my_col] + col_sum[my_row]
    for src, dst, mine, peer, sends, recvs, axis in copies:
        landed = remote(src.at[peer], dst.at[peer], sends.at[peer], recvs.at[peer], {axis: peer})
        landed.wait_send()
        landed.wait_recv()
        total = total + dst[peer]

    image = jnp.where(live, spread_ref[...] * total + var_ref[...] * masked_dir, 0.0)

    def lane_sum(values):
        return jnp.sum(jnp.sum(values, axis=0), axis=0, keepdims=True)

    for index, values in enumerate(
        (masked_res * masked_res, masked_dir * image, masked_res * image, image * image)
    ):
        mine_stats[pl.ds(index, 1), :] = lane_sum(values)
    stats[me] = mine_stats[...]

    for peer in peers:
        remote(mine_stats, stats.at[me], send_stat, recv_stat, peer).start()
    every = stats.at[pl.ds(0, device_count - 1)]
    pltpu.make_async_copy(every, every, send_stat).wait()
    pltpu.make_async_copy(every, every, recv_stat).wait()
    sums = jnp.sum(jnp.sum(stats[...], axis=0), axis=1, keepdims=True)
    res_norm, curvature, cross, image_norm = (sums[at : at + 1, :][None] for at in range(4))
    step_size = res_norm / curvature
    next_norm = res_norm - 2.0 * step_size * cross + step_size * step_size * image_norm
    residual_next = masked_res - step_size * image
    iter_out[...] = jnp.where(live, iter_ref[...], 0.0) + step_size * masked_dir
    res_out[...] = residual_next
    dir_out[...] = residual_next + next_norm / res_norm * masked_dir


def vmem(count):
    return [pl.BlockSpec(memory_space=pltpu.VMEM)] * count


def local(
    row_count, col_count, positions, region_cell, spread, obs_var, counts, pair_flags, iterate,
    residual, direction,
):
    local_rows, _, slots = spread.shape
    tiles = slots // LANES
    flat = (local_rows, tiles, LANES)
    device_count = row_count * col_count
    f32, i32 = jnp.float32, jnp.int32
    dma = pltpu.SemaphoreType.DMA
    spread_l, var_l, iter_l, res_l, dir_l = (
        value.reshape(flat) for value in (spread, obs_var, iterate, residual, direction)
    )
    grid_cells = device_count * local_rows
    row_part, col_part, meta = pl.pallas_call(
        functools.partial(gather_kernel, row_count, col_count),
        out_shape=(
            jax.ShapeDtypeStruct((col_count, 3, local_rows, tiles, LANES), f32),
            jax.ShapeDtypeStruct((row_count, 3, local_rows, tiles, LANES), f32),
            jax.ShapeDtypeStruct((device_count, 1, LANES), i32),
        ),
        in_specs=[pl.BlockSpec(memory_space=pltpu.HBM)] * 5,
        out_specs=tuple(vmem(3)),
        scratch_shapes=[
            pltpu.VMEM((local_rows, 2, slots), f32),
            pltpu.VMEM((1, local_rows), i32),
            pltpu.VMEM((1, local_rows), i32),
            pltpu.VMEM(flat, f32),
            pltpu.VMEM(flat, f32),
            dma((5,)),
            dma((row_count,)),
            dma((row_count,)),
            dma((col_count,)),
            dma((col_count,)),
            dma(()),
            dma(()),
        ],
        compiler_params=pltpu.CompilerParams(
            collective_id=0, has_side_effects=True, vmem_limit_bytes=VMEM_BYTES
        ),
        name="gather_parts",
    )(
        positions.reshape(local_rows, 2, slots),
        region_cell.reshape(1, local_rows),
        counts.reshape(1, local_rows),
        spread_l,
        dir_l,
    )

    row_sum, col_sum = pl.pallas_call(
        pair_kernel,
        out_shape=(
            jax.ShapeDtypeStruct((col_count, local_rows, tiles, LANES), f32),
            jax.ShapeDtypeStruct((row_count, local_rows, tiles, LANES), f32),
        ),
        in_specs=[pl.BlockSpec(memory_space=pltpu.SMEM)] + vmem(2),
        out_specs=tuple(vmem(2)),
        scratch_shapes=[
            pltpu.VMEM((tiles, 3, LANES, LANES), f32),
            pltpu.VMEM((tiles, LANES, LANES), f32),
            pltpu.VMEM((tiles, 8, LANES), f32),
            pltpu.VMEM((3, tiles, LANES), f32),
            pltpu.VMEM((3, tiles, LANES), f32),
            pltpu.VMEM((2, tiles, LANES), f32),
        ]
        + [pltpu.SMEM((grid_cells + col_count,), i32)] * 4
        + [pltpu.SMEM((device_count,), i32), pltpu.SMEM((5 * grid_cells + 1,), i32)],
        compiler_params=pltpu.CompilerParams(vmem_limit_bytes=VMEM_BYTES),
        name="pair_sums",
    )(meta.reshape(device_count, LANES), row_part, col_part)

    outs = pl.pallas_call(
        functools.partial(step_kernel, row_count, col_count),
        out_shape=(jax.ShapeDtypeStruct(flat, f32),) * 3,
        in_specs=vmem(8),
        out_specs=tuple(vmem(3)),
        scratch_shapes=[
            pltpu.VMEM((col_count, local_rows, tiles, LANES), f32),
            pltpu.VMEM((row_count, local_rows, tiles, LANES), f32),
            pltpu.VMEM((device_count, 4, LANES), f32),
            pltpu.VMEM((4, LANES), f32),
            dma((row_count,)),
            dma((row_count,)),
            dma((col_count,)),
            dma((col_count,)),
            dma(()),
            dma(()),
        ],
        compiler_params=pltpu.CompilerParams(
            collective_id=1, has_side_effects=True, vmem_limit_bytes=VMEM_BYTES
        ),
        name="reduce_and_step",
    )(row_sum, col_sum, meta, spread_l, var_l, dir_l, res_l, iter_l)
    return tuple(out.reshape(spread.shape) for out in outs)


def solution(mesh):
    per_slot = P(("groups", "rows"), "cols", None)
    return jax.shard_map(
        functools.partial(local, mesh.shape["rows"], mesh.shape["cols"]),
        mesh=mesh,
        in_specs=(
            P(("groups", "rows"), "cols", None, None),
            P(("groups", "rows"), "cols"),
            per_slot,
            per_slot,
            P(("groups", "rows"), "cols"),
            P(("groups", "rows"), None, None, "cols"),
            per_slot,
            per_slot,
            per_slot,
        ),
        out_specs=(per_slot, per_slot, per_slot),
        check_vma=False,
    )
```

```python
import functools
import math

import jax
import jax.numpy as jnp
from jax import lax
from jax.experimental import pallas as pl
from jax.experimental.pallas import tpu as pltpu
from jax.sharding import PartitionSpec as P

ROOT_THREE = 1.7320508075688772
MATERN_LENGTH = 0.5
RATE = ROOT_THREE / MATERN_LENGTH
MESH = pl.DeviceIdType.MESH
LANES = 128
CHUNK = 32
BITS = RATE / math.log(2.0)
SCALE = 4.0 * RATE * BITS**-6 * 2.0**-BITS
TILE_COST, OWN_COST, PAIR_COST = 100, 220, 150
FIELD = 1 << 15
VMEM_BYTES = 40 * 1024 * 1024


def remote(src, dst, send_sem, recv_sem, device):
    return pltpu.make_async_remote_copy(
        src_ref=src,
        dst_ref=dst,
        send_sem=send_sem,
        recv_sem=recv_sem,
        device_id=device,
        device_id_type=MESH,
    )


def slot_numbers(shape):
    tile_at = lax.broadcasted_iota(jnp.int32, shape, 1)
    return tile_at * LANES + lax.broadcasted_iota(jnp.int32, shape, 2)


def others(row_count, col_count):
    my_row, my_col = lax.axis_index("rows"), lax.axis_index("cols")
    rows = [lax.rem(my_row + step, row_count) for step in range(row_count)]
    cols = [lax.rem(my_col + step, col_count) for step in range(col_count)]
    return [{"rows": row, "cols": col} for row in rows for col in cols][1:]


def greet_all(peers):
    barrier = pltpu.get_barrier_semaphore()
    for peer in peers:
        pl.semaphore_signal(barrier, inc=1, device_id=peer, device_id_type=MESH)
    return barrier


def gather_kernel(
    row_count, col_count, pos_hbm, cell_hbm, count_hbm, spread_hbm, dir_hbm,
    row_out, col_out, meta_out, pos_ref, cell_ref, count_ref, spread_ref, dir_ref, local_sem,
    send_row, recv_row, send_col, recv_col, send_meta, recv_meta,
):
    my_row, my_col = lax.axis_index("rows"), lax.axis_index("cols")
    row_peers = [lax.rem(my_row + step, row_count) for step in range(1, row_count)]
    col_peers = [lax.rem(my_col + step, col_count) for step in range(1, col_count)]
    device_count = row_count * col_count
    me = my_row * col_count + my_col
    loads = [
        pltpu.make_async_copy(src, dst, local_sem.at[index])
        for index, (src, dst) in enumerate(
            (
                (cell_hbm, cell_ref),
                (count_hbm, count_ref),
                (pos_hbm, pos_ref),
                (spread_hbm, spread_ref),
                (dir_hbm, dir_ref),
            )
        )
    ]
    for load in loads:
        load.start()
    peers = others(row_count, col_count)
    barrier = greet_all(peers)

    local_rows, tiles, _ = spread_ref.shape
    for load in loads:
        load.wait()
    lane_at = lax.broadcasted_iota(jnp.int32, (1, LANES), 1)
    slot_at = slot_numbers((1, tiles, LANES))[0]
    meta = jnp.zeros((1, LANES), jnp.int32)
    for line in range(local_rows):
        count = count_ref[:, line : line + 1]
        cell = cell_ref[:, line : line + 1]
        meta = jnp.where(lane_at == 2 * line, count, meta)
        meta = jnp.where(lane_at == 2 * line + 1, cell, meta)
        cell = cell.astype(jnp.float32)
        cell_row = jnp.floor((cell + 0.5) * (1.0 / col_count))
        cell_col = cell - cell_row * col_count
        weighted = spread_ref[line] * jnp.where(slot_at < count, dir_ref[line], 0.0)
        row_out[my_col, 2, line] = weighted
        col_out[my_row, 2, line] = weighted
        for axis, corner in enumerate((cell_row, cell_col)):
            for tile in range(tiles):
                span = slice(tile * LANES, (tile + 1) * LANES)
                located = pos_ref[line, axis : axis + 1, span] + corner
                row_out[my_col, axis, line, tile : tile + 1, :] = located
                col_out[my_row, axis, line, tile : tile + 1, :] = located
    meta_out[me] = meta
    pl.semaphore_wait(barrier, device_count - 1)

    copies = []
    for peer in row_peers:
        copies.append((col_out, my_row, peer, send_row, recv_row, "rows"))
    for peer in col_peers:
        copies.append((row_out, my_col, peer, send_col, recv_col, "cols"))
    for ref, mine, peer, sends, recvs, axis in copies:
        remote(ref.at[mine], ref.at[mine], sends.at[peer], recvs.at[mine], {axis: peer}).start()
    for peer in peers:
        remote(meta_out.at[me], meta_out.at[me], send_meta, recv_meta, peer).start()
    every = meta_out.at[pl.ds(0, device_count - 1)]
    pltpu.make_async_copy(every, every, send_meta).wait()
    pltpu.make_async_copy(every, every, recv_meta).wait()
    for ref, mine, peer, sends, recvs, axis in copies:
        landed = remote(ref.at[mine], ref.at[peer], sends.at[peer], recvs.at[peer], {axis: peer})
        landed.wait_send()
        landed.wait_recv()


def covariance(delta_x, delta_y):
    square = jnp.maximum(delta_x * delta_x + delta_y * delta_y, 1e-30)
    scaled = square * lax.rsqrt(square)
    gap = jnp.maximum(BITS - scaled, 0.0)
    power = jnp.exp2(gap)
    gap = gap * gap
    gap = gap * gap
    growth = (scaled + BITS / 4.0) * (scaled + BITS / RATE)
    return growth * gap * power


def tile_count(slots):
    return lax.shift_right_logical(slots + (LANES - 1), LANES.bit_length() - 1)


def choose_pairs(meta, cell_tiles, cell_row, cell_col, cell_line, load, chosen, sizes):
    row_count, col_count, local_rows = sizes
    grid_rows = row_count * local_rows
    me = lax.axis_index("rows") * col_count + lax.axis_index("cols")

    def cost(first_tiles, second_tiles):
        least = jnp.minimum(first_tiles, second_tiles)
        return TILE_COST * first_tiles * second_tiles + OWN_COST * least + PAIR_COST

    def place_regions(row, carry):
        for col in range(col_count):
            device = row * col_count + col
            total = 0
            for line in range(local_rows):
                cell = meta[device, 2 * line + 1]
                tiles = tile_count(meta[device, 2 * line])
                cell_tiles[cell] = tiles
                cell_row[cell] = row * col_count
                cell_col[cell] = col
                cell_line[cell] = line
                total = total + cost(tiles, tiles)
            load[device] = total
        return carry

    lax.fori_loop(0, row_count, place_regions, 0)
    for col in range(col_count):
        past = grid_rows * col_count + col
        cell_tiles[past] = 0
        cell_row[past] = 0
        cell_col[past] = 0
        cell_line[past] = 0
    for line in range(local_rows):
        chosen[line] = meta[me, 2 * line + 1] * (FIELD + 1)

    def near_cells(row, total):
        for col in range(col_count):
            first = row * col_count + col
            first_tiles, first_row, first_col = cell_tiles[first], cell_row[first], cell_col[first]
            for down, across in ((0, 1), (1, -1), (1, 0), (1, 1)):
                if not 0 <= col + across < col_count:
                    continue
                second = first + down * col_count + across
                second_tiles = cell_tiles[second]
                present = second_tiles > 0
                forward = first_row + cell_col[second]
                backward = cell_row[second] + first_col
                work = jnp.where(present, cost(first_tiles, second_tiles), 0)
                forward_load, backward_load = load[forward], load[backward]
                ahead = forward_load <= backward_load
                device = jnp.where(ahead, forward, backward)
                load[device] = jnp.minimum(forward_load, backward_load) + work
                chosen[total] = jnp.where(
                    ahead, first * FIELD + second, second * FIELD + first
                )
                total = total + jnp.where((device == me) & present, 1, 0)
        return total

    return lax.fori_loop(0, grid_rows, near_cells, local_rows)


def pair_kernel(
    meta, row_ref, col_ref, row_sum, col_sum, own_wide, own_acc, other_acc,
    own_local, other_local, sums, cell_tiles, cell_row, cell_col, cell_line, load, chosen,
):
    col_count, _, local_rows, tiles, _ = row_ref.shape
    row_count = col_ref.shape[0]
    row_sum[...] = jnp.zeros_like(row_sum)
    col_sum[...] = jnp.zeros_like(col_sum)
    total = choose_pairs(
        meta, cell_tiles, cell_row, cell_col, cell_line, load, chosen,
        (row_count, col_count, local_rows),
    )

    def places(index):
        pair = chosen[index]
        row_cell = lax.shift_right_logical(pair, FIELD.bit_length() - 1)
        col_cell = pair & (FIELD - 1)
        row_at = cell_col[row_cell], cell_line[row_cell]
        col_at = lax.div(cell_row[col_cell], col_count), cell_line[col_cell]
        row_tiles, col_tiles = cell_tiles[row_cell], cell_tiles[col_cell]
        return row_at, col_at, row_tiles, col_tiles, row_cell == col_cell

    def spread_out(tile):
        for plane in range(3):
            line = jnp.broadcast_to(own_local[plane, pl.ds(tile, 1), :], (LANES, LANES))
            own_wide[tile, plane] = line.T

    def set_up(index):
        (row_group, row_line), (col_group, col_line), row_tiles, col_tiles, same = places(index)
        swap = col_tiles < row_tiles
        keep = jnp.where(same, 0.0, SCALE)
        whole = pl.ds(0, tiles)
        for axis in range(2):
            origin = row_ref[row_group, axis, row_line, 0:1, 0:1]
            row_axis = (row_ref[row_group, axis, row_line] - origin) * BITS
            col_axis = (col_ref[col_group, axis, col_line] - origin) * BITS
            own_local[axis, whole] = jnp.where(swap, col_axis, row_axis)
            other_local[axis] = jnp.where(swap, row_axis, col_axis)
        row_weight = row_ref[row_group, 2, row_line] * keep
        col_weight = col_ref[col_group, 2, col_line] * SCALE
        own_local[2, whole] = jnp.where(swap, col_weight, row_weight)
        other_local[2] = jnp.where(swap, row_weight, col_weight)
        other_acc[...] = jnp.zeros_like(other_acc)
        spread_out(0)

    def close_tile(tile):
        sums[pl.ds(tile + 1, 1), :] = jnp.sum(own_acc[tile + 1].T, axis=0, keepdims=True)

    def one_pair(index, carry):
        (row_group, row_line), (col_group, col_line), row_tiles, col_tiles, _ = places(index)
        swap = col_tiles < row_tiles
        own_tiles = jnp.minimum(row_tiles, col_tiles)
        other_tiles = jnp.maximum(row_tiles, col_tiles)

        def own_tile(tile, inner):
            def body(first, width, fresh):
                lines = [
                    [other_local[plane, pl.ds(first + step, 1), :] for plane in range(3)]
                    for step in range(width)
                ]
                totals = [other_acc[first + step] for step in range(width)]
                for start in range(0, LANES, CHUNK):
                    part = pl.ds(start, CHUNK)
                    part_x, part_y, part_w = (own_wide[tile, plane, part, :] for plane in range(3))
                    part_acc = 0.0 if fresh else own_acc[tile + 1, part, :]
                    for step in range(width):
                        line_x, line_y, line_w = lines[step]
                        value = covariance(part_x - line_x, part_y - line_y)
                        part_acc = part_acc + value * line_w
                        backward = value * part_w
                        totals[step] = totals[step] + jnp.sum(
                            backward.reshape(CHUNK // 8, 8, LANES), axis=0
                        )
                    own_acc[tile + 1, part, :] = part_acc
                for step in range(width):
                    other_acc[first + step] = totals[step]

            def first_body(width):
                close_tile(tile - 1)
                spread_out(tile + 1)
                body(0, width, True)

            odd = other_tiles & 1

            @pl.when(odd == 1)
            def _():
                first_body(1)

            @pl.when(odd == 0)
            def _():
                first_body(2)

            def two(pair, nested):
                body(pair * 2 + odd, 2, False)
                return nested

            lax.fori_loop(1 - odd, lax.shift_right_logical(other_tiles, 1), two, 0)
            return inner

        lax.fori_loop(0, own_tiles, own_tile, 0)
        close_tile(own_tiles - 1)
        other_sum = jnp.sum(other_acc[...], axis=1)
        shown = lax.broadcasted_iota(jnp.int32, (tiles, LANES), 0) < own_tiles
        own_sum = jnp.where(shown, sums[pl.ds(1, tiles), :], 0.0)
        row_sum[row_group, row_line] += jnp.where(swap, other_sum, own_sum)
        col_sum[col_group, col_line] += jnp.where(swap, own_sum, other_sum)
        set_up(jnp.minimum(index + 1, total - 1))
        return carry

    own_local[...] = jnp.zeros_like(own_local)
    own_acc[0] = jnp.zeros_like(own_acc[0])
    set_up(0)
    lax.fori_loop(0, total, one_pair, 0)


def step_kernel(
    row_count, col_count, row_sum, col_sum, meta_ref, spread_ref, var_ref, dir_ref, res_ref,
    iter_ref, iter_out, res_out, dir_out, row_land, col_land, stats, mine_stats,
    send_row, recv_row, send_col, recv_col, send_stat, recv_stat,
):
    my_row, my_col = lax.axis_index("rows"), lax.axis_index("cols")
    device_count = row_count * col_count
    me = my_row * col_count + my_col
    row_peers = [lax.rem(my_row + step, row_count) for step in range(1, row_count)]
    col_peers = [lax.rem(my_col + step, col_count) for step in range(1, col_count)]
    peers = others(row_count, col_count)
    barrier = greet_all(peers)
    local_rows = spread_ref.shape[0]
    meta = meta_ref[me]
    line_at = lax.broadcasted_iota(jnp.int32, spread_ref.shape, 0)
    counts = jnp.zeros(spread_ref.shape, jnp.int32)
    for line in range(local_rows):
        counts = jnp.where(line_at == line, meta[:, 2 * line : 2 * line + 1][None], counts)
    live = slot_numbers(spread_ref.shape) < counts
    masked_dir = jnp.where(live, dir_ref[...], 0.0)
    masked_res = jnp.where(live, res_ref[...], 0.0)
    pl.semaphore_wait(barrier, device_count - 1)

    copies = []
    for peer in row_peers:
        copies.append((col_sum, col_land, my_row, peer, send_row, recv_row, "rows"))
    for peer in col_peers:
        copies.append((row_sum, row_land, my_col, peer, send_col, recv_col, "cols"))
    for src, dst, mine, peer, sends, recvs, axis in copies:
        remote(src.at[peer], dst.at[mine], sends.at[peer], recvs.at[mine], {axis: peer}).start()
    total = row_sum[my_col] + col_sum[my_row]
    for src, dst, mine, peer, sends, recvs, axis in copies:
        landed = remote(src.at[peer], dst.at[peer], sends.at[peer], recvs.at[peer], {axis: peer})
        landed.wait_send()
        landed.wait_recv()
        total = total + dst[peer]

    image = jnp.where(live, spread_ref[...] * total + var_ref[...] * masked_dir, 0.0)

    def lane_sum(values):
        return jnp.sum(jnp.sum(values, axis=0), axis=0, keepdims=True)

    for index, values in enumerate(
        (masked_res * masked_res, masked_dir * image, masked_res * image, image * image)
    ):
        mine_stats[pl.ds(index, 1), :] = lane_sum(values)
    stats[me] = mine_stats[...]

    for peer in peers:
        remote(mine_stats, stats.at[me], send_stat, recv_stat, peer).start()
    every = stats.at[pl.ds(0, device_count - 1)]
    pltpu.make_async_copy(every, every, send_stat).wait()
    pltpu.make_async_copy(every, every, recv_stat).wait()
    sums = jnp.sum(jnp.sum(stats[...], axis=0), axis=1, keepdims=True)
    res_norm, curvature, cross, image_norm = (sums[at : at + 1, :][None] for at in range(4))
    step_size = res_norm / curvature
    next_norm = res_norm - 2.0 * step_size * cross + step_size * step_size * image_norm
    residual_next = masked_res - step_size * image
    iter_out[...] = jnp.where(live, iter_ref[...], 0.0) + step_size * masked_dir
    res_out[...] = residual_next
    dir_out[...] = residual_next + next_norm / res_norm * masked_dir


def vmem(count):
    return [pl.BlockSpec(memory_space=pltpu.VMEM)] * count


def local(
    row_count, col_count, positions, region_cell, spread, obs_var, counts, pair_flags, iterate,
    residual, direction,
):
    local_rows, _, slots = spread.shape
    tiles = slots // LANES
    flat = (local_rows, tiles, LANES)
    device_count = row_count * col_count
    f32, i32 = jnp.float32, jnp.int32
    dma = pltpu.SemaphoreType.DMA
    spread_l, var_l, iter_l, res_l, dir_l = (
        value.reshape(flat) for value in (spread, obs_var, iterate, residual, direction)
    )
    grid_cells = device_count * local_rows
    row_part, col_part, meta = pl.pallas_call(
        functools.partial(gather_kernel, row_count, col_count),
        out_shape=(
            jax.ShapeDtypeStruct((col_count, 3, local_rows, tiles, LANES), f32),
            jax.ShapeDtypeStruct((row_count, 3, local_rows, tiles, LANES), f32),
            jax.ShapeDtypeStruct((device_count, 1, LANES), i32),
        ),
        in_specs=[pl.BlockSpec(memory_space=pltpu.HBM)] * 5,
        out_specs=tuple(vmem(3)),
        scratch_shapes=[
            pltpu.VMEM((local_rows, 2, slots), f32),
            pltpu.VMEM((1, local_rows), i32),
            pltpu.VMEM((1, local_rows), i32),
            pltpu.VMEM(flat, f32),
            pltpu.VMEM(flat, f32),
            dma((5,)),
            dma((row_count,)),
            dma((row_count,)),
            dma((col_count,)),
            dma((col_count,)),
            dma(()),
            dma(()),
        ],
        compiler_params=pltpu.CompilerParams(
            collective_id=0, has_side_effects=True, vmem_limit_bytes=VMEM_BYTES
        ),
        name="gather_parts",
    )(
        positions.reshape(local_rows, 2, slots),
        region_cell.reshape(1, local_rows),
        counts.reshape(1, local_rows),
        spread_l,
        dir_l,
    )

    row_sum, col_sum = pl.pallas_call(
        pair_kernel,
        out_shape=(
            jax.ShapeDtypeStruct((col_count, local_rows, tiles, LANES), f32),
            jax.ShapeDtypeStruct((row_count, local_rows, tiles, LANES), f32),
        ),
        in_specs=[pl.BlockSpec(memory_space=pltpu.SMEM)] + vmem(2),
        out_specs=tuple(vmem(2)),
        scratch_shapes=[
            pltpu.VMEM((tiles + 1, 3, LANES, LANES), f32),
            pltpu.VMEM((tiles + 1, LANES, LANES), f32),
            pltpu.VMEM((tiles, 8, LANES), f32),
            pltpu.VMEM((3, tiles + 8, LANES), f32),
            pltpu.VMEM((3, tiles, LANES), f32),
            pltpu.VMEM((tiles + 8, LANES), f32),
        ]
        + [pltpu.SMEM((grid_cells + col_count,), i32)] * 4
        + [pltpu.SMEM((device_count,), i32), pltpu.SMEM((5 * grid_cells + 1,), i32)],
        compiler_params=pltpu.CompilerParams(vmem_limit_bytes=VMEM_BYTES),
        name="pair_sums",
    )(meta.reshape(device_count, LANES), row_part, col_part)

    outs = pl.pallas_call(
        functools.partial(step_kernel, row_count, col_count),
        out_shape=(jax.ShapeDtypeStruct(flat, f32),) * 3,
        in_specs=vmem(8),
        out_specs=tuple(vmem(3)),
        scratch_shapes=[
            pltpu.VMEM((col_count, local_rows, tiles, LANES), f32),
            pltpu.VMEM((row_count, local_rows, tiles, LANES), f32),
            pltpu.VMEM((device_count, 4, LANES), f32),
            pltpu.VMEM((4, LANES), f32),
            dma((row_count,)),
            dma((row_count,)),
            dma((col_count,)),
            dma((col_count,)),
            dma(()),
            dma(()),
        ],
        compiler_params=pltpu.CompilerParams(
            collective_id=1, has_side_effects=True, vmem_limit_bytes=VMEM_BYTES
        ),
        name="reduce_and_step",
    )(row_sum, col_sum, meta, spread_l, var_l, dir_l, res_l, iter_l)
    return tuple(out.reshape(spread.shape) for out in outs)


def solution(mesh):
    per_slot = P(("groups", "rows"), "cols", None)
    return jax.shard_map(
        functools.partial(local, mesh.shape["rows"], mesh.shape["cols"]),
        mesh=mesh,
        in_specs=(
            P(("groups", "rows"), "cols", None, None),
            P(("groups", "rows"), "cols"),
            per_slot,
            per_slot,
            P(("groups", "rows"), "cols"),
            P(("groups", "rows"), None, None, "cols"),
            per_slot,
            per_slot,
            per_slot,
        ),
        out_specs=(per_slot, per_slot, per_slot),
        check_vma=False,
    )
```

```python
import functools
import math

import jax
import jax.numpy as jnp
from jax import lax
from jax.experimental import pallas as pl
from jax.experimental.pallas import tpu as pltpu
from jax.sharding import PartitionSpec as P

ROOT_THREE = 1.7320508075688772
MATERN_LENGTH = 0.5
RATE = ROOT_THREE / MATERN_LENGTH
MESH = pl.DeviceIdType.MESH
LANES = 128
CHUNK = 32
BITS = RATE / math.log(2.0)
SCALE = 4.0 * RATE * BITS**-6 * 2.0**-BITS
TILE_COST, OWN_COST, PAIR_COST = 100, 90, 120
FIELD = 1 << 15
VMEM_BYTES = 40 * 1024 * 1024


def remote(src, dst, send_sem, recv_sem, device):
    return pltpu.make_async_remote_copy(
        src_ref=src,
        dst_ref=dst,
        send_sem=send_sem,
        recv_sem=recv_sem,
        device_id=device,
        device_id_type=MESH,
    )


def slot_numbers(shape):
    tile_at = lax.broadcasted_iota(jnp.int32, shape, 1)
    return tile_at * LANES + lax.broadcasted_iota(jnp.int32, shape, 2)


def others(row_count, col_count):
    my_row, my_col = lax.axis_index("rows"), lax.axis_index("cols")
    rows = [lax.rem(my_row + step, row_count) for step in range(row_count)]
    cols = [lax.rem(my_col + step, col_count) for step in range(col_count)]
    return [{"rows": row, "cols": col} for row in rows for col in cols][1:]


def greet_all(peers):
    barrier = pltpu.get_barrier_semaphore()
    for peer in peers:
        pl.semaphore_signal(barrier, inc=1, device_id=peer, device_id_type=MESH)
    return barrier


def gather_kernel(
    row_count, col_count, pos_hbm, cell_hbm, count_hbm, spread_hbm, dir_hbm,
    row_out, col_out, meta_out, pos_ref, cell_ref, count_ref, spread_ref, dir_ref, local_sem,
    send_row, recv_row, send_col, recv_col, send_meta, recv_meta,
):
    my_row, my_col = lax.axis_index("rows"), lax.axis_index("cols")
    row_peers = [lax.rem(my_row + step, row_count) for step in range(1, row_count)]
    col_peers = [lax.rem(my_col + step, col_count) for step in range(1, col_count)]
    device_count = row_count * col_count
    me = my_row * col_count + my_col
    loads = [
        pltpu.make_async_copy(src, dst, local_sem.at[index])
        for index, (src, dst) in enumerate(
            (
                (cell_hbm, cell_ref),
                (count_hbm, count_ref),
                (pos_hbm, pos_ref),
                (spread_hbm, spread_ref),
                (dir_hbm, dir_ref),
            )
        )
    ]
    for load in loads:
        load.start()
    peers = others(row_count, col_count)
    barrier = greet_all(peers)

    local_rows, tiles, _ = spread_ref.shape
    for load in loads:
        load.wait()
    lane_at = lax.broadcasted_iota(jnp.int32, (1, LANES), 1)
    slot_at = slot_numbers((1, tiles, LANES))[0]
    meta = jnp.zeros((1, LANES), jnp.int32)
    for line in range(local_rows):
        count = count_ref[:, line : line + 1]
        cell = cell_ref[:, line : line + 1]
        meta = jnp.where(lane_at == 2 * line, count, meta)
        meta = jnp.where(lane_at == 2 * line + 1, cell, meta)
        cell = cell.astype(jnp.float32)
        cell_row = jnp.floor((cell + 0.5) * (1.0 / col_count))
        cell_col = cell - cell_row * col_count
        weighted = spread_ref[line] * jnp.where(slot_at < count, dir_ref[line], 0.0)
        row_out[my_col, 2, line] = weighted
        col_out[my_row, 2, line] = weighted
        for axis, corner in enumerate((cell_row, cell_col)):
            for tile in range(tiles):
                span = slice(tile * LANES, (tile + 1) * LANES)
                located = pos_ref[line, axis : axis + 1, span] + corner
                row_out[my_col, axis, line, tile : tile + 1, :] = located
                col_out[my_row, axis, line, tile : tile + 1, :] = located
    meta_out[me] = meta
    pl.semaphore_wait(barrier, device_count - 1)

    copies = []
    for peer in row_peers:
        copies.append((col_out, my_row, peer, send_row, recv_row, "rows"))
    for peer in col_peers:
        copies.append((row_out, my_col, peer, send_col, recv_col, "cols"))
    for ref, mine, peer, sends, recvs, axis in copies:
        remote(ref.at[mine], ref.at[mine], sends.at[peer], recvs.at[mine], {axis: peer}).start()
    for peer in peers:
        remote(meta_out.at[me], meta_out.at[me], send_meta, recv_meta, peer).start()
    every = meta_out.at[pl.ds(0, device_count - 1)]
    pltpu.make_async_copy(every, every, send_meta).wait()
    pltpu.make_async_copy(every, every, recv_meta).wait()
    for ref, mine, peer, sends, recvs, axis in copies:
        landed = remote(ref.at[mine], ref.at[peer], sends.at[peer], recvs.at[peer], {axis: peer})
        landed.wait_send()
        landed.wait_recv()


def covariance(delta_x, delta_y):
    square = jnp.maximum(delta_x * delta_x + delta_y * delta_y, 1e-30)
    scaled = square * lax.rsqrt(square)
    gap = jnp.maximum(BITS - scaled, 0.0)
    power = jnp.exp2(gap)
    gap = gap * gap
    gap = gap * gap
    growth = (scaled + BITS / 4.0) * (scaled + BITS / RATE)
    return growth * gap * power


def tile_count(slots):
    return lax.shift_right_logical(slots + (LANES - 1), LANES.bit_length() - 1)


def choose_pairs(meta, cell_tiles, cell_row, cell_col, cell_line, load, chosen, sizes):
    row_count, col_count, local_rows = sizes
    grid_rows = row_count * local_rows
    me = lax.axis_index("rows") * col_count + lax.axis_index("cols")

    def cost(first_tiles, second_tiles):
        least = jnp.minimum(first_tiles, second_tiles)
        return TILE_COST * first_tiles * second_tiles + OWN_COST * least + PAIR_COST

    def place_regions(row, carry):
        for col in range(col_count):
            device = row * col_count + col
            total = 0
            for line in range(local_rows):
                cell = meta[device, 2 * line + 1]
                tiles = tile_count(meta[device, 2 * line])
                cell_tiles[cell] = tiles
                cell_row[cell] = row * col_count
                cell_col[cell] = col
                cell_line[cell] = line
                total = total + cost(tiles, tiles)
            load[device] = total
        return carry

    lax.fori_loop(0, row_count, place_regions, 0)
    for col in range(col_count):
        past = grid_rows * col_count + col
        cell_tiles[past] = 0
        cell_row[past] = 0
        cell_col[past] = 0
        cell_line[past] = 0
    for line in range(local_rows):
        chosen[line] = meta[me, 2 * line + 1] * (FIELD + 1)

    def near_cells(row, total):
        for col in range(col_count):
            first = row * col_count + col
            first_tiles, first_row, first_col = cell_tiles[first], cell_row[first], cell_col[first]
            for down, across in ((0, 1), (1, -1), (1, 0), (1, 1)):
                if not 0 <= col + across < col_count:
                    continue
                second = first + down * col_count + across
                second_tiles = cell_tiles[second]
                present = second_tiles > 0
                forward = first_row + cell_col[second]
                backward = cell_row[second] + first_col
                work = jnp.where(present, cost(first_tiles, second_tiles), 0)
                forward_load, backward_load = load[forward], load[backward]
                ahead = forward_load <= backward_load
                device = jnp.where(ahead, forward, backward)
                load[device] = jnp.minimum(forward_load, backward_load) + work
                chosen[total] = jnp.where(
                    ahead, first * FIELD + second, second * FIELD + first
                )
                total = total + jnp.where((device == me) & present, 1, 0)
        return total

    return lax.fori_loop(0, grid_rows, near_cells, local_rows)


def pair_kernel(
    meta, row_ref, col_ref, sums, own_wide, own_acc, other_acc, own_local, other_local,
    cell_tiles, cell_row, cell_col, cell_line, load, chosen,
):
    col_count, _, local_rows, tiles, _ = row_ref.shape
    row_count = col_ref.shape[0]
    sums[...] = jnp.zeros_like(sums)
    total = choose_pairs(
        meta, cell_tiles, cell_row, cell_col, cell_line, load, chosen,
        (row_count, col_count, local_rows),
    )

    def places(index):
        pair = chosen[index]
        row_cell = lax.shift_right_logical(pair, FIELD.bit_length() - 1)
        col_cell = pair & (FIELD - 1)
        row_at = cell_col[row_cell], cell_line[row_cell]
        col_at = lax.div(cell_row[col_cell], col_count), cell_line[col_cell]
        row_tiles, col_tiles = cell_tiles[row_cell], cell_tiles[col_cell]
        return row_at, col_at, row_tiles, col_tiles, row_cell == col_cell

    def spread_out(buffer, tile, slot):
        for plane in range(3):
            line = own_local[buffer, plane, pl.ds(tile, 1), :]
            own_wide[slot, plane] = jnp.broadcast_to(line, (LANES, LANES)).T

    def set_up(index, buffer):
        (row_group, row_line), (col_group, col_line), row_tiles, col_tiles, same = places(index)
        swap = col_tiles < row_tiles
        keep = jnp.where(same, 0.0, SCALE)
        for axis in range(2):
            origin = row_ref[row_group, axis, row_line, 0:1, 0:1]
            row_axis = (row_ref[row_group, axis, row_line] - origin) * BITS
            col_axis = (col_ref[col_group, axis, col_line] - origin) * BITS
            own_local[buffer, axis] = jnp.where(swap, col_axis, row_axis)
            other_local[buffer, axis] = jnp.where(swap, row_axis, col_axis)
        row_weight = row_ref[row_group, 2, row_line] * keep
        col_weight = col_ref[col_group, 2, col_line] * SCALE
        own_local[buffer, 2] = jnp.where(swap, col_weight, row_weight)
        other_local[buffer, 2] = jnp.where(swap, row_weight, col_weight)

    def close_tile(slot, group, line, tile):
        sums[group, line, pl.ds(tile, 1), :] += jnp.sum(own_acc[slot].T, axis=0, keepdims=True)

    def one_pair(index, carry):
        start, last_group, last_line, last_tile = carry
        (row_group, row_line), (col_group, col_line), row_tiles, col_tiles, _ = places(index)
        swap = col_tiles < row_tiles
        own_tiles = jnp.minimum(row_tiles, col_tiles)
        other_tiles = jnp.maximum(row_tiles, col_tiles)
        own_group = jnp.where(swap, col_count + col_group, row_group)
        own_line = jnp.where(swap, col_line, row_line)
        other_group = jnp.where(swap, row_group, col_count + col_group)
        other_line = jnp.where(swap, row_line, col_line)
        buffer = index & 1
        set_up(jnp.minimum(index + 1, total - 1), 1 - buffer)

        def own_tile(tile, inner):
            last_group, last_line, last_tile = inner
            slot = start + tile

            def body(first, width, fresh):
                lines = [
                    [other_local[buffer, plane, pl.ds(first + step, 1), :] for plane in range(3)]
                    for step in range(width)
                ]
                totals = [other_acc[first + step] for step in range(width)]
                for at in range(0, LANES, CHUNK):
                    part = pl.ds(at, CHUNK)
                    part_x, part_y, part_w = (own_wide[slot, plane, part, :] for plane in range(3))
                    part_acc = 0.0 if fresh else own_acc[slot + 1, part, :]
                    for step in range(width):
                        line_x, line_y, line_w = lines[step]
                        value = covariance(part_x - line_x, part_y - line_y)
                        part_acc = part_acc + value * line_w
                        backward = value * part_w
                        totals[step] = totals[step] + jnp.sum(
                            backward.reshape(CHUNK // 8, 8, LANES), axis=0
                        )
                    own_acc[slot + 1, part, :] = part_acc
                for step in range(width):
                    other_acc[first + step] = totals[step]

            ends = tile + 1 >= own_tiles
            next_buffer = jnp.where(ends, 1 - buffer, buffer)
            next_tile = jnp.where(ends, 0, tile + 1)

            def first_body(width):
                close_tile(slot, last_group, last_line, last_tile)
                spread_out(next_buffer, next_tile, slot + 1)
                body(0, width, True)

            odd = other_tiles & 1

            @pl.when(odd == 1)
            def _():
                first_body(1)

            @pl.when(odd == 0)
            def _():
                first_body(2)

            def two(pair, nested):
                body(pair * 2 + odd, 2, False)
                return nested

            lax.fori_loop(1 - odd, lax.shift_right_logical(other_tiles, 1), two, 0)
            return own_group, own_line, tile

        last = lax.fori_loop(0, own_tiles, own_tile, (last_group, last_line, last_tile))
        start = start + own_tiles
        wrap = start > tiles

        @pl.when(wrap)
        def _():
            own_wide[0] = own_wide[start]
            own_acc[0] = own_acc[start]

        sums[other_group, other_line] += jnp.sum(other_acc[...], axis=1)
        other_acc[...] = jnp.zeros_like(other_acc)
        return jnp.where(wrap, 0, start), *last

    other_acc[...] = jnp.zeros_like(other_acc)
    own_acc[0] = jnp.zeros_like(own_acc[0])
    set_up(0, 0)
    spread_out(0, 0, 0)
    start, last_group, last_line, last_tile = lax.fori_loop(0, total, one_pair, (0, 0, 0, 0))
    close_tile(start, last_group, last_line, last_tile)


def step_kernel(
    row_count, col_count, sum_ref, meta_ref, spread_ref, var_ref, dir_ref, res_ref,
    iter_ref, iter_out, res_out, dir_out, row_land, col_land, stats, mine_stats,
    send_row, recv_row, send_col, recv_col, send_stat, recv_stat,
):
    my_row, my_col = lax.axis_index("rows"), lax.axis_index("cols")
    device_count = row_count * col_count
    me = my_row * col_count + my_col
    row_peers = [lax.rem(my_row + step, row_count) for step in range(1, row_count)]
    col_peers = [lax.rem(my_col + step, col_count) for step in range(1, col_count)]
    peers = others(row_count, col_count)
    barrier = greet_all(peers)
    local_rows = spread_ref.shape[0]
    meta = meta_ref[me]
    line_at = lax.broadcasted_iota(jnp.int32, spread_ref.shape, 0)
    counts = jnp.zeros(spread_ref.shape, jnp.int32)
    for line in range(local_rows):
        counts = jnp.where(line_at == line, meta[:, 2 * line : 2 * line + 1][None], counts)
    live = slot_numbers(spread_ref.shape) < counts
    masked_dir = jnp.where(live, dir_ref[...], 0.0)
    masked_res = jnp.where(live, res_ref[...], 0.0)
    pl.semaphore_wait(barrier, device_count - 1)

    copies = []
    for peer in row_peers:
        copies.append((col_count, col_land, my_row, peer, send_row, recv_row, "rows"))
    for peer in col_peers:
        copies.append((0, row_land, my_col, peer, send_col, recv_col, "cols"))
    for base, dst, mine, peer, sends, recvs, axis in copies:
        src = sum_ref.at[base + peer]
        remote(src, dst.at[mine], sends.at[peer], recvs.at[mine], {axis: peer}).start()
    total = sum_ref[my_col] + sum_ref[col_count + my_row]
    for base, dst, mine, peer, sends, recvs, axis in copies:
        src = sum_ref.at[base + peer]
        landed = remote(src, dst.at[peer], sends.at[peer], recvs.at[peer], {axis: peer})
        landed.wait_send()
        landed.wait_recv()
        total = total + dst[peer]

    image = jnp.where(live, spread_ref[...] * total + var_ref[...] * masked_dir, 0.0)

    def lane_sum(values):
        return jnp.sum(jnp.sum(values, axis=0), axis=0, keepdims=True)

    for index, values in enumerate(
        (masked_res * masked_res, masked_dir * image, masked_res * image, image * image)
    ):
        mine_stats[pl.ds(index, 1), :] = lane_sum(values)
    stats[me] = mine_stats[...]

    for peer in peers:
        remote(mine_stats, stats.at[me], send_stat, recv_stat, peer).start()
    every = stats.at[pl.ds(0, device_count - 1)]
    pltpu.make_async_copy(every, every, send_stat).wait()
    pltpu.make_async_copy(every, every, recv_stat).wait()
    sums = jnp.sum(jnp.sum(stats[...], axis=0), axis=1, keepdims=True)
    res_norm, curvature, cross, image_norm = (sums[at : at + 1, :][None] for at in range(4))
    step_size = res_norm / curvature
    next_norm = res_norm - 2.0 * step_size * cross + step_size * step_size * image_norm
    residual_next = masked_res - step_size * image
    iter_out[...] = jnp.where(live, iter_ref[...], 0.0) + step_size * masked_dir
    res_out[...] = residual_next
    dir_out[...] = residual_next + next_norm / res_norm * masked_dir


def vmem(count):
    return [pl.BlockSpec(memory_space=pltpu.VMEM)] * count


def local(
    row_count, col_count, positions, region_cell, spread, obs_var, counts, pair_flags, iterate,
    residual, direction,
):
    local_rows, _, slots = spread.shape
    tiles = slots // LANES
    flat = (local_rows, tiles, LANES)
    device_count = row_count * col_count
    f32, i32 = jnp.float32, jnp.int32
    dma = pltpu.SemaphoreType.DMA
    spread_l, var_l, iter_l, res_l, dir_l = (
        value.reshape(flat) for value in (spread, obs_var, iterate, residual, direction)
    )
    grid_cells = device_count * local_rows
    row_part, col_part, meta = pl.pallas_call(
        functools.partial(gather_kernel, row_count, col_count),
        out_shape=(
            jax.ShapeDtypeStruct((col_count, 3, local_rows, tiles, LANES), f32),
            jax.ShapeDtypeStruct((row_count, 3, local_rows, tiles, LANES), f32),
            jax.ShapeDtypeStruct((device_count, 1, LANES), i32),
        ),
        in_specs=[pl.BlockSpec(memory_space=pltpu.HBM)] * 5,
        out_specs=tuple(vmem(3)),
        scratch_shapes=[
            pltpu.VMEM((local_rows, 2, slots), f32),
            pltpu.VMEM((1, local_rows), i32),
            pltpu.VMEM((1, local_rows), i32),
            pltpu.VMEM(flat, f32),
            pltpu.VMEM(flat, f32),
            dma((5,)),
            dma((row_count,)),
            dma((row_count,)),
            dma((col_count,)),
            dma((col_count,)),
            dma(()),
            dma(()),
        ],
        compiler_params=pltpu.CompilerParams(
            collective_id=0, has_side_effects=True, vmem_limit_bytes=VMEM_BYTES
        ),
        name="gather_parts",
    )(
        positions.reshape(local_rows, 2, slots),
        region_cell.reshape(1, local_rows),
        counts.reshape(1, local_rows),
        spread_l,
        dir_l,
    )

    sums = pl.pallas_call(
        pair_kernel,
        out_shape=jax.ShapeDtypeStruct((col_count + row_count, local_rows, tiles, LANES), f32),
        in_specs=[pl.BlockSpec(memory_space=pltpu.SMEM)] + vmem(2),
        out_specs=vmem(1)[0],
        scratch_shapes=[
            pltpu.VMEM((2 * tiles + 1, 3, LANES, LANES), f32),
            pltpu.VMEM((2 * tiles + 1, LANES, LANES), f32),
            pltpu.VMEM((tiles, 8, LANES), f32),
            pltpu.VMEM((2, 3, tiles, LANES), f32),
            pltpu.VMEM((2, 3, tiles, LANES), f32),
        ]
        + [pltpu.SMEM((grid_cells + col_count,), i32)] * 4
        + [pltpu.SMEM((device_count,), i32), pltpu.SMEM((5 * grid_cells + 1,), i32)],
        compiler_params=pltpu.CompilerParams(vmem_limit_bytes=VMEM_BYTES),
        name="pair_sums",
    )(meta.reshape(device_count, LANES), row_part, col_part)

    outs = pl.pallas_call(
        functools.partial(step_kernel, row_count, col_count),
        out_shape=(jax.ShapeDtypeStruct(flat, f32),) * 3,
        in_specs=vmem(7),
        out_specs=tuple(vmem(3)),
        scratch_shapes=[
            pltpu.VMEM((col_count, local_rows, tiles, LANES), f32),
            pltpu.VMEM((row_count, local_rows, tiles, LANES), f32),
            pltpu.VMEM((device_count, 4, LANES), f32),
            pltpu.VMEM((4, LANES), f32),
            dma((row_count,)),
            dma((row_count,)),
            dma((col_count,)),
            dma((col_count,)),
            dma(()),
            dma(()),
        ],
        compiler_params=pltpu.CompilerParams(
            collective_id=1, has_side_effects=True, vmem_limit_bytes=VMEM_BYTES
        ),
        name="reduce_and_step",
    )(sums, meta, spread_l, var_l, dir_l, res_l, iter_l)
    return tuple(out.reshape(spread.shape) for out in outs)


def solution(mesh):
    per_slot = P(("groups", "rows"), "cols", None)
    return jax.shard_map(
        functools.partial(local, mesh.shape["rows"], mesh.shape["cols"]),
        mesh=mesh,
        in_specs=(
            P(("groups", "rows"), "cols", None, None),
            P(("groups", "rows"), "cols"),
            per_slot,
            per_slot,
            P(("groups", "rows"), "cols"),
            P(("groups", "rows"), None, None, "cols"),
            per_slot,
            per_slot,
            per_slot,
        ),
        out_specs=(per_slot, per_slot, per_slot),
        check_vma=False,
    )
```

```python
import functools
import math

import jax
import jax.numpy as jnp
from jax import lax
from jax.experimental import pallas as pl
from jax.experimental.pallas import tpu as pltpu
from jax.sharding import PartitionSpec as P

ROOT_THREE = 1.7320508075688772
MATERN_LENGTH = 0.5
RATE = ROOT_THREE / MATERN_LENGTH
MESH = pl.DeviceIdType.MESH
LANES = 128
CHUNK = 32
BITS = RATE / math.log(2.0)
SCALE = 4.0 * RATE * BITS**-6 * 2.0**-BITS
TILE_COST, OWN_COST, PAIR_COST = 100, 90, 120
FIELD = 1 << 15
VMEM_BYTES = 40 * 1024 * 1024


def remote(src, dst, send_sem, recv_sem, device):
    return pltpu.make_async_remote_copy(
        src_ref=src,
        dst_ref=dst,
        send_sem=send_sem,
        recv_sem=recv_sem,
        device_id=device,
        device_id_type=MESH,
    )


def slot_numbers(shape):
    tile_at = lax.broadcasted_iota(jnp.int32, shape, 1)
    return tile_at * LANES + lax.broadcasted_iota(jnp.int32, shape, 2)


def others(row_count, col_count):
    my_row, my_col = lax.axis_index("rows"), lax.axis_index("cols")
    rows = [lax.rem(my_row + step, row_count) for step in range(row_count)]
    cols = [lax.rem(my_col + step, col_count) for step in range(col_count)]
    return [{"rows": row, "cols": col} for row in rows for col in cols][1:]


def greet_all(peers):
    barrier = pltpu.get_barrier_semaphore()
    for peer in peers:
        pl.semaphore_signal(barrier, inc=1, device_id=peer, device_id_type=MESH)
    return barrier


def gather_kernel(
    row_count, col_count, part_hbm, cell_hbm, count_hbm,
    row_out, col_out, meta_out, part_ref, cell_ref, count_ref, local_sem,
    send_row, recv_row, send_col, recv_col, send_meta, recv_meta,
):
    my_row, my_col = lax.axis_index("rows"), lax.axis_index("cols")
    row_peers = [lax.rem(my_row + step, row_count) for step in range(1, row_count)]
    col_peers = [lax.rem(my_col + step, col_count) for step in range(1, col_count)]
    device_count = row_count * col_count
    me = my_row * col_count + my_col
    loads = [
        pltpu.make_async_copy(src, dst, local_sem.at[index])
        for index, (src, dst) in enumerate(
            (
                (cell_hbm, cell_ref),
                (count_hbm, count_ref),
                (part_hbm, part_ref),
            )
        )
    ]
    for load in loads:
        load.start()
    peers = others(row_count, col_count)
    barrier = greet_all(peers)

    local_rows, tiles = row_out.shape[2:4]
    for load in loads:
        load.wait()
    lane_at = lax.broadcasted_iota(jnp.int32, (1, LANES), 1)
    slot_at = slot_numbers((1, tiles, LANES))[0]
    meta = jnp.zeros((1, LANES), jnp.int32)
    for line in range(local_rows):
        count = count_ref[:, line : line + 1]
        cell = cell_ref[:, line : line + 1]
        meta = jnp.where(lane_at == 2 * line, count, meta)
        meta = jnp.where(lane_at == 2 * line + 1, cell, meta)
        cell = cell.astype(jnp.float32)
        cell_row = jnp.floor((cell + 0.5) * (1.0 / col_count))
        cell_col = cell - cell_row * col_count
        for tile in range(tiles):
            span = slice(tile * LANES, (tile + 1) * LANES)
            first, second, spread, turn = (part_ref[line, at : at + 1, span] for at in range(4))
            live = slot_at[tile : tile + 1] < count
            planes = first + cell_row, second + cell_col, spread * jnp.where(live, turn, 0.0)
            for index, plane in enumerate(planes):
                row_out[my_col, index, line, tile : tile + 1, :] = plane
                col_out[my_row, index, line, tile : tile + 1, :] = plane
    meta_out[me] = meta
    pl.semaphore_wait(barrier, device_count - 1)

    copies = []
    for peer in row_peers:
        copies.append((col_out, my_row, peer, send_row, recv_row, "rows"))
    for peer in col_peers:
        copies.append((row_out, my_col, peer, send_col, recv_col, "cols"))
    for ref, mine, peer, sends, recvs, axis in copies:
        remote(ref.at[mine], ref.at[mine], sends.at[peer], recvs.at[mine], {axis: peer}).start()
    for peer in peers:
        remote(meta_out.at[me], meta_out.at[me], send_meta, recv_meta, peer).start()
    every = meta_out.at[pl.ds(0, device_count - 1)]
    pltpu.make_async_copy(every, every, send_meta).wait()
    pltpu.make_async_copy(every, every, recv_meta).wait()
    for ref, mine, peer, sends, recvs, axis in copies:
        landed = remote(ref.at[mine], ref.at[peer], sends.at[peer], recvs.at[peer], {axis: peer})
        landed.wait_send()
        landed.wait_recv()


def covariance(delta_x, delta_y):
    square = jnp.maximum(delta_x * delta_x + delta_y * delta_y, 1e-30)
    scaled = square * lax.rsqrt(square)
    gap = jnp.maximum(BITS - scaled, 0.0)
    power = jnp.exp2(gap)
    gap = gap * gap
    gap = gap * gap
    growth = (scaled + BITS / 4.0) * (scaled + BITS / RATE)
    return growth * gap * power


def tile_count(slots):
    return lax.shift_right_logical(slots + (LANES - 1), LANES.bit_length() - 1)


def choose_pairs(meta, cell_tiles, cell_row, cell_col, cell_line, load, chosen, sizes):
    row_count, col_count, local_rows = sizes
    grid_rows = row_count * local_rows
    me = lax.axis_index("rows") * col_count + lax.axis_index("cols")

    def cost(first_tiles, second_tiles):
        least = jnp.minimum(first_tiles, second_tiles)
        return TILE_COST * first_tiles * second_tiles + OWN_COST * least + PAIR_COST

    def place_regions(row, carry):
        for col in range(col_count):
            device = row * col_count + col
            total = 0
            for line in range(local_rows):
                cell = meta[device, 2 * line + 1]
                tiles = tile_count(meta[device, 2 * line])
                cell_tiles[cell] = tiles
                cell_row[cell] = row * col_count
                cell_col[cell] = col
                cell_line[cell] = line
                total = total + cost(tiles, tiles)
            load[device] = total
        return carry

    lax.fori_loop(0, row_count, place_regions, 0)
    for col in range(col_count):
        past = grid_rows * col_count + col
        cell_tiles[past] = 0
        cell_row[past] = 0
        cell_col[past] = 0
        cell_line[past] = 0
    for line in range(local_rows):
        chosen[line] = meta[me, 2 * line + 1] * (FIELD + 1)

    def near_cells(row, total):
        for col in range(col_count):
            first = row * col_count + col
            first_tiles, first_row, first_col = cell_tiles[first], cell_row[first], cell_col[first]
            for down, across in ((0, 1), (1, -1), (1, 0), (1, 1)):
                if not 0 <= col + across < col_count:
                    continue
                second = first + down * col_count + across
                second_tiles = cell_tiles[second]
                present = second_tiles > 0
                forward = first_row + cell_col[second]
                backward = cell_row[second] + first_col
                work = jnp.where(present, cost(first_tiles, second_tiles), 0)
                forward_load, backward_load = load[forward], load[backward]
                ahead = forward_load <= backward_load
                device = jnp.where(ahead, forward, backward)
                load[device] = jnp.minimum(forward_load, backward_load) + work
                chosen[total] = jnp.where(
                    ahead, first * FIELD + second, second * FIELD + first
                )
                total = total + jnp.where((device == me) & present, 1, 0)
        return total

    return lax.fori_loop(0, grid_rows, near_cells, local_rows)


def pair_kernel(
    meta, row_ref, col_ref, sums, own_wide, own_acc, other_acc, own_local, other_local,
    cell_tiles, cell_row, cell_col, cell_line, load, chosen,
):
    col_count, _, local_rows, tiles, _ = row_ref.shape
    row_count = col_ref.shape[0]
    sums[...] = jnp.zeros_like(sums)
    total = choose_pairs(
        meta, cell_tiles, cell_row, cell_col, cell_line, load, chosen,
        (row_count, col_count, local_rows),
    )

    def places(index):
        pair = chosen[index]
        row_cell = lax.shift_right_logical(pair, FIELD.bit_length() - 1)
        col_cell = pair & (FIELD - 1)
        row_at = cell_col[row_cell], cell_line[row_cell]
        col_at = lax.div(cell_row[col_cell], col_count), cell_line[col_cell]
        row_tiles, col_tiles = cell_tiles[row_cell], cell_tiles[col_cell]
        return row_at, col_at, row_tiles, col_tiles, row_cell == col_cell

    def spread_out(buffer, tile, slot):
        for plane in range(3):
            line = own_local[buffer, plane, pl.ds(tile, 1), :]
            own_wide[slot, plane] = jnp.broadcast_to(line, (LANES, LANES)).T

    def set_up(index, buffer):
        (row_group, row_line), (col_group, col_line), row_tiles, col_tiles, same = places(index)
        swap = col_tiles < row_tiles
        keep = jnp.where(same, 0.0, SCALE)
        for axis in range(2):
            origin = row_ref[row_group, axis, row_line, 0:1, 0:1]
            row_axis = (row_ref[row_group, axis, row_line] - origin) * BITS
            col_axis = (col_ref[col_group, axis, col_line] - origin) * BITS
            own_local[buffer, axis] = jnp.where(swap, col_axis, row_axis)
            other_local[buffer, axis] = jnp.where(swap, row_axis, col_axis)
        row_weight = row_ref[row_group, 2, row_line] * keep
        col_weight = col_ref[col_group, 2, col_line] * SCALE
        own_local[buffer, 2] = jnp.where(swap, col_weight, row_weight)
        other_local[buffer, 2] = jnp.where(swap, row_weight, col_weight)

    def close_tile(slot, group, line, tile):
        sums[group, line, pl.ds(tile, 1), :] += jnp.sum(own_acc[slot].T, axis=0, keepdims=True)

    def one_pair(index, carry):
        start, last_group, last_line, last_tile = carry
        (row_group, row_line), (col_group, col_line), row_tiles, col_tiles, _ = places(index)
        swap = col_tiles < row_tiles
        own_tiles = jnp.minimum(row_tiles, col_tiles)
        other_tiles = jnp.maximum(row_tiles, col_tiles)
        own_group = jnp.where(swap, col_count + col_group, row_group)
        own_line = jnp.where(swap, col_line, row_line)
        other_group = jnp.where(swap, row_group, col_count + col_group)
        other_line = jnp.where(swap, row_line, col_line)
        buffer = index & 1
        set_up(jnp.minimum(index + 1, total - 1), 1 - buffer)

        def own_tile(tile, inner):
            last_group, last_line, last_tile = inner
            slot = start + tile

            def body(first, width, fresh):
                lines = [
                    [other_local[buffer, plane, pl.ds(first + step, 1), :] for plane in range(3)]
                    for step in range(width)
                ]
                totals = [other_acc[first + step] for step in range(width)]
                for at in range(0, LANES, CHUNK):
                    part = pl.ds(at, CHUNK)
                    part_x, part_y, part_w = (own_wide[slot, plane, part, :] for plane in range(3))
                    part_acc = 0.0 if fresh else own_acc[slot + 1, part, :]
                    for step in range(width):
                        line_x, line_y, line_w = lines[step]
                        value = covariance(part_x - line_x, part_y - line_y)
                        part_acc = part_acc + value * line_w
                        backward = value * part_w
                        totals[step] = totals[step] + jnp.sum(
                            backward.reshape(CHUNK // 8, 8, LANES), axis=0
                        )
                    own_acc[slot + 1, part, :] = part_acc
                for step in range(width):
                    other_acc[first + step] = totals[step]

            ends = tile + 1 >= own_tiles
            next_buffer = jnp.where(ends, 1 - buffer, buffer)
            next_tile = jnp.where(ends, 0, tile + 1)

            def first_body(width):
                close_tile(slot, last_group, last_line, last_tile)
                spread_out(next_buffer, next_tile, slot + 1)
                body(0, width, True)

            odd = other_tiles & 1

            @pl.when(odd == 1)
            def _():
                first_body(1)

            @pl.when(odd == 0)
            def _():
                first_body(2)

            def two(pair, nested):
                body(pair * 2 + odd, 2, False)
                return nested

            lax.fori_loop(1 - odd, lax.shift_right_logical(other_tiles, 1), two, 0)
            return own_group, own_line, tile

        last = lax.fori_loop(0, own_tiles, own_tile, (last_group, last_line, last_tile))
        start = start + own_tiles
        wrap = start > tiles

        @pl.when(wrap)
        def _():
            own_wide[0] = own_wide[start]
            own_acc[0] = own_acc[start]

        sums[other_group, other_line] += jnp.sum(other_acc[...], axis=1)
        other_acc[...] = jnp.zeros_like(other_acc)
        return jnp.where(wrap, 0, start), *last

    other_acc[...] = jnp.zeros_like(other_acc)
    own_acc[0] = jnp.zeros_like(own_acc[0])
    set_up(0, 0)
    spread_out(0, 0, 0)
    start, last_group, last_line, last_tile = lax.fori_loop(0, total, one_pair, (0, 0, 0, 0))
    close_tile(start, last_group, last_line, last_tile)


def step_kernel(
    row_count, col_count, sum_ref, meta_ref, spread_ref, var_ref, dir_ref, res_ref,
    iter_ref, iter_out, res_out, dir_out, row_land, col_land, stats, mine_stats,
    send_row, recv_row, send_col, recv_col, send_stat, recv_stat,
):
    my_row, my_col = lax.axis_index("rows"), lax.axis_index("cols")
    device_count = row_count * col_count
    me = my_row * col_count + my_col
    row_peers = [lax.rem(my_row + step, row_count) for step in range(1, row_count)]
    col_peers = [lax.rem(my_col + step, col_count) for step in range(1, col_count)]
    peers = others(row_count, col_count)
    barrier = greet_all(peers)
    local_rows = spread_ref.shape[0]
    meta = meta_ref[me]
    line_at = lax.broadcasted_iota(jnp.int32, spread_ref.shape, 0)
    counts = jnp.zeros(spread_ref.shape, jnp.int32)
    for line in range(local_rows):
        counts = jnp.where(line_at == line, meta[:, 2 * line : 2 * line + 1][None], counts)
    live = slot_numbers(spread_ref.shape) < counts
    masked_dir = jnp.where(live, dir_ref[...], 0.0)
    masked_res = jnp.where(live, res_ref[...], 0.0)
    pl.semaphore_wait(barrier, device_count - 1)

    copies = []
    for peer in row_peers:
        copies.append((col_count, col_land, my_row, peer, send_row, recv_row, "rows"))
    for peer in col_peers:
        copies.append((0, row_land, my_col, peer, send_col, recv_col, "cols"))
    for base, dst, mine, peer, sends, recvs, axis in copies:
        src = sum_ref.at[base + peer]
        remote(src, dst.at[mine], sends.at[peer], recvs.at[mine], {axis: peer}).start()
    total = sum_ref[my_col] + sum_ref[col_count + my_row]
    for base, dst, mine, peer, sends, recvs, axis in copies:
        src = sum_ref.at[base + peer]
        landed = remote(src, dst.at[peer], sends.at[peer], recvs.at[peer], {axis: peer})
        landed.wait_send()
        landed.wait_recv()
        total = total + dst[peer]

    image = jnp.where(live, spread_ref[...] * total + var_ref[...] * masked_dir, 0.0)

    def lane_sum(values):
        return jnp.sum(jnp.sum(values, axis=0), axis=0, keepdims=True)

    for index, values in enumerate(
        (masked_res * masked_res, masked_dir * image, masked_res * image, image * image)
    ):
        mine_stats[pl.ds(index, 1), :] = lane_sum(values)
    stats[me] = mine_stats[...]

    for peer in peers:
        remote(mine_stats, stats.at[me], send_stat, recv_stat, peer).start()
    every = stats.at[pl.ds(0, device_count - 1)]
    pltpu.make_async_copy(every, every, send_stat).wait()
    pltpu.make_async_copy(every, every, recv_stat).wait()
    sums = jnp.sum(jnp.sum(stats[...], axis=0), axis=1, keepdims=True)
    res_norm, curvature, cross, image_norm = (sums[at : at + 1, :][None] for at in range(4))
    step_size = res_norm / curvature
    next_norm = res_norm - 2.0 * step_size * cross + step_size * step_size * image_norm
    residual_next = masked_res - step_size * image
    iter_out[...] = jnp.where(live, iter_ref[...], 0.0) + step_size * masked_dir
    res_out[...] = residual_next
    dir_out[...] = residual_next + next_norm / res_norm * masked_dir


def vmem(count):
    return [pl.BlockSpec(memory_space=pltpu.VMEM)] * count


def local(
    row_count, col_count, positions, region_cell, spread, obs_var, counts, pair_flags, iterate,
    residual, direction,
):
    local_rows, _, slots = spread.shape
    tiles = slots // LANES
    flat = (local_rows, tiles, LANES)
    device_count = row_count * col_count
    f32, i32 = jnp.float32, jnp.int32
    dma = pltpu.SemaphoreType.DMA
    spread_l, var_l, iter_l, res_l, dir_l = (
        value.reshape(flat) for value in (spread, obs_var, iterate, residual, direction)
    )
    grid_cells = device_count * local_rows
    row_part, col_part, meta = pl.pallas_call(
        functools.partial(gather_kernel, row_count, col_count),
        out_shape=(
            jax.ShapeDtypeStruct((col_count, 3, local_rows, tiles, LANES), f32),
            jax.ShapeDtypeStruct((row_count, 3, local_rows, tiles, LANES), f32),
            jax.ShapeDtypeStruct((device_count, 1, LANES), i32),
        ),
        in_specs=[pl.BlockSpec(memory_space=pltpu.HBM)] * 3,
        out_specs=tuple(vmem(3)),
        scratch_shapes=[
            pltpu.VMEM((local_rows, 4, slots), f32),
            pltpu.VMEM((1, local_rows), i32),
            pltpu.VMEM((1, local_rows), i32),
            dma((3,)),
            dma((row_count,)),
            dma((row_count,)),
            dma((col_count,)),
            dma((col_count,)),
            dma(()),
            dma(()),
        ],
        compiler_params=pltpu.CompilerParams(
            collective_id=0, has_side_effects=True, vmem_limit_bytes=VMEM_BYTES
        ),
        name="gather_parts",
    )(
        jnp.concatenate([positions.reshape(local_rows, 2, slots), spread, direction], axis=1),
        region_cell.reshape(1, local_rows),
        counts.reshape(1, local_rows),
    )

    sums = pl.pallas_call(
        pair_kernel,
        out_shape=jax.ShapeDtypeStruct((col_count + row_count, local_rows, tiles, LANES), f32),
        in_specs=[pl.BlockSpec(memory_space=pltpu.SMEM)] + vmem(2),
        out_specs=vmem(1)[0],
        scratch_shapes=[
            pltpu.VMEM((2 * tiles + 1, 3, LANES, LANES), f32),
            pltpu.VMEM((2 * tiles + 1, LANES, LANES), f32),
            pltpu.VMEM((tiles, 8, LANES), f32),
            pltpu.VMEM((2, 3, tiles, LANES), f32),
            pltpu.VMEM((2, 3, tiles, LANES), f32),
        ]
        + [pltpu.SMEM((grid_cells + col_count,), i32)] * 4
        + [pltpu.SMEM((device_count,), i32), pltpu.SMEM((5 * grid_cells + 1,), i32)],
        compiler_params=pltpu.CompilerParams(vmem_limit_bytes=VMEM_BYTES),
        name="pair_sums",
    )(meta.reshape(device_count, LANES), row_part, col_part)

    outs = pl.pallas_call(
        functools.partial(step_kernel, row_count, col_count),
        out_shape=(jax.ShapeDtypeStruct(flat, f32),) * 3,
        in_specs=vmem(7),
        out_specs=tuple(vmem(3)),
        scratch_shapes=[
            pltpu.VMEM((col_count, local_rows, tiles, LANES), f32),
            pltpu.VMEM((row_count, local_rows, tiles, LANES), f32),
            pltpu.VMEM((device_count, 4, LANES), f32),
            pltpu.VMEM((4, LANES), f32),
            dma((row_count,)),
            dma((row_count,)),
            dma((col_count,)),
            dma((col_count,)),
            dma(()),
            dma(()),
        ],
        compiler_params=pltpu.CompilerParams(
            collective_id=1, has_side_effects=True, vmem_limit_bytes=VMEM_BYTES
        ),
        name="reduce_and_step",
    )(sums, meta, spread_l, var_l, dir_l, res_l, iter_l)
    return tuple(out.reshape(spread.shape) for out in outs)


def solution(mesh):
    per_slot = P(("groups", "rows"), "cols", None)
    return jax.shard_map(
        functools.partial(local, mesh.shape["rows"], mesh.shape["cols"]),
        mesh=mesh,
        in_specs=(
            P(("groups", "rows"), "cols", None, None),
            P(("groups", "rows"), "cols"),
            per_slot,
            per_slot,
            P(("groups", "rows"), "cols"),
            P(("groups", "rows"), None, None, "cols"),
            per_slot,
            per_slot,
            per_slot,
        ),
        out_specs=(per_slot, per_slot, per_slot),
        check_vma=False,
    )
```

```python
import functools
import math

import jax
import jax.numpy as jnp
from jax import lax
from jax.experimental import pallas as pl
from jax.experimental.pallas import tpu as pltpu
from jax.sharding import PartitionSpec as P

ROOT_THREE = 1.7320508075688772
MATERN_LENGTH = 0.5
RATE = ROOT_THREE / MATERN_LENGTH
MESH = pl.DeviceIdType.MESH
LANES = 128
CHUNK = 32
BITS = RATE / math.log(2.0)
SCALE = 4.0 * RATE * BITS**-6 * 2.0**-BITS
TILE_COST, OWN_COST, PAIR_COST = 100, 90, 120
FIELD = 1 << 15
VMEM_BYTES = 40 * 1024 * 1024


def remote(src, dst, send_sem, recv_sem, device):
    return pltpu.make_async_remote_copy(
        src_ref=src,
        dst_ref=dst,
        send_sem=send_sem,
        recv_sem=recv_sem,
        device_id=device,
        device_id_type=MESH,
    )


def slot_numbers(shape):
    tile_at = lax.broadcasted_iota(jnp.int32, shape, 1)
    return tile_at * LANES + lax.broadcasted_iota(jnp.int32, shape, 2)


def others(row_count, col_count):
    my_row, my_col = lax.axis_index("rows"), lax.axis_index("cols")
    rows = [lax.rem(my_row + step, row_count) for step in range(row_count)]
    cols = [lax.rem(my_col + step, col_count) for step in range(col_count)]
    return [{"rows": row, "cols": col} for row in rows for col in cols][1:]


def greet_all(peers):
    barrier = pltpu.get_barrier_semaphore()
    for peer in peers:
        pl.semaphore_signal(barrier, inc=1, device_id=peer, device_id_type=MESH)
    return barrier


def gather_kernel(
    row_count, col_count, part_hbm, cell_hbm, count_hbm,
    row_out, col_out, meta_out, part_ref, cell_ref, count_ref, local_sem,
    send_row, recv_row, send_col, recv_col, send_meta, recv_meta,
):
    my_row, my_col = lax.axis_index("rows"), lax.axis_index("cols")
    row_peers = [lax.rem(my_row + step, row_count) for step in range(1, row_count)]
    col_peers = [lax.rem(my_col + step, col_count) for step in range(1, col_count)]
    device_count = row_count * col_count
    me = my_row * col_count + my_col
    loads = [
        pltpu.make_async_copy(src, dst, local_sem.at[index])
        for index, (src, dst) in enumerate(
            (
                (cell_hbm, cell_ref),
                (count_hbm, count_ref),
                (part_hbm, part_ref),
            )
        )
    ]
    for load in loads:
        load.start()
    peers = others(row_count, col_count)
    barrier = greet_all(peers)

    local_rows, tiles = row_out.shape[2:4]
    for load in loads:
        load.wait()
    lane_at = lax.broadcasted_iota(jnp.int32, (1, LANES), 1)
    slot_at = slot_numbers((1, tiles, LANES))[0]
    meta = jnp.zeros((1, LANES), jnp.int32)
    for line in range(local_rows):
        count = count_ref[:, line : line + 1]
        cell = cell_ref[:, line : line + 1]
        meta = jnp.where(lane_at == 2 * line, count, meta)
        meta = jnp.where(lane_at == 2 * line + 1, cell, meta)
        cell = cell.astype(jnp.float32)
        cell_row = jnp.floor((cell + 0.5) * (1.0 / col_count))
        cell_col = cell - cell_row * col_count
        for tile in range(tiles):
            span = slice(tile * LANES, (tile + 1) * LANES)
            first, second, spread, turn = (part_ref[line, at : at + 1, span] for at in range(4))
            live = slot_at[tile : tile + 1] < count
            planes = first + cell_row, second + cell_col, spread * jnp.where(live, turn, 0.0)
            for index, plane in enumerate(planes):
                row_out[my_col, index, line, tile : tile + 1, :] = plane
                col_out[my_row, index, line, tile : tile + 1, :] = plane
    meta_out[me] = meta
    pl.semaphore_wait(barrier, device_count - 1)

    copies = []
    for peer in row_peers:
        copies.append((col_out, my_row, peer, send_row, recv_row, "rows"))
    for peer in col_peers:
        copies.append((row_out, my_col, peer, send_col, recv_col, "cols"))
    for peer in peers:
        remote(meta_out.at[me], meta_out.at[me], send_meta, recv_meta, peer).start()
    for ref, mine, peer, sends, recvs, axis in copies:
        remote(ref.at[mine], ref.at[mine], sends.at[peer], recvs.at[mine], {axis: peer}).start()
    every = meta_out.at[pl.ds(0, device_count - 1)]
    pltpu.make_async_copy(every, every, send_meta).wait()
    pltpu.make_async_copy(every, every, recv_meta).wait()
    for ref, mine, peer, sends, recvs, axis in copies:
        landed = remote(ref.at[mine], ref.at[peer], sends.at[peer], recvs.at[peer], {axis: peer})
        landed.wait_send()
        landed.wait_recv()


def covariance(delta_x, delta_y):
    square = jnp.maximum(delta_x * delta_x + delta_y * delta_y, 1e-30)
    scaled = square * lax.rsqrt(square)
    gap = jnp.maximum(BITS - scaled, 0.0)
    power = jnp.exp2(gap)
    gap = gap * gap
    gap = gap * gap
    growth = (scaled + BITS / 4.0) * (scaled + BITS / RATE)
    return growth * gap * power


def tile_count(slots):
    return lax.shift_right_logical(slots + (LANES - 1), LANES.bit_length() - 1)


def choose_pairs(meta, cell_tiles, cell_row, cell_col, cell_line, load, chosen, sizes):
    row_count, col_count, local_rows = sizes
    grid_rows = row_count * local_rows
    me = lax.axis_index("rows") * col_count + lax.axis_index("cols")

    def cost(first_tiles, second_tiles):
        least = jnp.minimum(first_tiles, second_tiles)
        return TILE_COST * first_tiles * second_tiles + OWN_COST * least + PAIR_COST

    def place_regions(row, carry):
        for col in range(col_count):
            device = row * col_count + col
            total = 0
            for line in range(local_rows):
                cell = meta[device, 2 * line + 1]
                tiles = tile_count(meta[device, 2 * line])
                cell_tiles[cell] = tiles
                cell_row[cell] = row * col_count
                cell_col[cell] = col
                cell_line[cell] = line
                total = total + cost(tiles, tiles)
            load[device] = total
        return carry

    lax.fori_loop(0, row_count, place_regions, 0)
    for col in range(col_count):
        past = grid_rows * col_count + col
        cell_tiles[past] = 0
        cell_row[past] = 0
        cell_col[past] = 0
        cell_line[past] = 0
    for line in range(local_rows):
        chosen[line] = meta[me, 2 * line + 1] * (FIELD + 1)

    def near_cells(row, total):
        for col in range(col_count):
            first = row * col_count + col
            first_tiles, first_row, first_col = cell_tiles[first], cell_row[first], cell_col[first]
            for down, across in ((0, 1), (1, -1), (1, 0), (1, 1)):
                if not 0 <= col + across < col_count:
                    continue
                second = first + down * col_count + across
                second_tiles = cell_tiles[second]
                present = second_tiles > 0
                forward = first_row + cell_col[second]
                backward = cell_row[second] + first_col
                work = jnp.where(present, cost(first_tiles, second_tiles), 0)
                forward_load, backward_load = load[forward], load[backward]
                ahead = forward_load <= backward_load
                device = jnp.where(ahead, forward, backward)
                load[device] = jnp.minimum(forward_load, backward_load) + work
                chosen[total] = jnp.where(
                    ahead, first * FIELD + second, second * FIELD + first
                )
                total = total + jnp.where((device == me) & present, 1, 0)
        return total

    return lax.fori_loop(0, grid_rows, near_cells, local_rows)


def pair_kernel(
    meta, row_ref, col_ref, sums, own_wide, own_acc, other_acc, own_local, other_local,
    cell_tiles, cell_row, cell_col, cell_line, load, chosen,
):
    col_count, _, local_rows, tiles, _ = row_ref.shape
    row_count = col_ref.shape[0]
    sums[...] = jnp.zeros_like(sums)
    total = choose_pairs(
        meta, cell_tiles, cell_row, cell_col, cell_line, load, chosen,
        (row_count, col_count, local_rows),
    )

    def places(index):
        pair = chosen[index]
        row_cell = lax.shift_right_logical(pair, FIELD.bit_length() - 1)
        col_cell = pair & (FIELD - 1)
        row_at = cell_col[row_cell], cell_line[row_cell]
        col_at = lax.div(cell_row[col_cell], col_count), cell_line[col_cell]
        row_tiles, col_tiles = cell_tiles[row_cell], cell_tiles[col_cell]
        return row_at, col_at, row_tiles, col_tiles, row_cell == col_cell

    def spread_out(buffer, tile, slot):
        for plane in range(3):
            line = own_local[buffer, plane, pl.ds(tile, 1), :]
            own_wide[slot, plane] = jnp.broadcast_to(line, (LANES, LANES)).T

    def set_up(index, buffer):
        (row_group, row_line), (col_group, col_line), row_tiles, col_tiles, same = places(index)
        swap = col_tiles < row_tiles
        keep = jnp.where(same, 0.0, SCALE)
        for axis in range(2):
            origin = row_ref[row_group, axis, row_line, 0:1, 0:1]
            row_axis = (row_ref[row_group, axis, row_line] - origin) * BITS
            col_axis = (col_ref[col_group, axis, col_line] - origin) * BITS
            own_local[buffer, axis] = jnp.where(swap, col_axis, row_axis)
            other_local[buffer, axis] = jnp.where(swap, row_axis, col_axis)
        row_weight = row_ref[row_group, 2, row_line] * keep
        col_weight = col_ref[col_group, 2, col_line] * SCALE
        own_local[buffer, 2] = jnp.where(swap, col_weight, row_weight)
        other_local[buffer, 2] = jnp.where(swap, row_weight, col_weight)

    def close_tile(slot, group, line, tile):
        sums[group, line, pl.ds(tile, 1), :] += jnp.sum(own_acc[slot].T, axis=0, keepdims=True)

    def one_pair(index, carry):
        start, last_group, last_line, last_tile = carry
        (row_group, row_line), (col_group, col_line), row_tiles, col_tiles, _ = places(index)
        swap = col_tiles < row_tiles
        own_tiles = jnp.minimum(row_tiles, col_tiles)
        other_tiles = jnp.maximum(row_tiles, col_tiles)
        own_group = jnp.where(swap, col_count + col_group, row_group)
        own_line = jnp.where(swap, col_line, row_line)
        other_group = jnp.where(swap, row_group, col_count + col_group)
        other_line = jnp.where(swap, row_line, col_line)
        buffer = index & 1
        set_up(jnp.minimum(index + 1, total - 1), 1 - buffer)

        def own_tile(tile, inner):
            last_group, last_line, last_tile = inner
            slot = start + tile

            def body(first, width, fresh):
                lines = [
                    [other_local[buffer, plane, pl.ds(first + step, 1), :] for plane in range(3)]
                    for step in range(width)
                ]
                totals = [other_acc[first + step] for step in range(width)]
                for at in range(0, LANES, CHUNK):
                    part = pl.ds(at, CHUNK)
                    part_x, part_y, part_w = (own_wide[slot, plane, part, :] for plane in range(3))
                    part_acc = 0.0 if fresh else own_acc[slot + 1, part, :]
                    for step in range(width):
                        line_x, line_y, line_w = lines[step]
                        value = covariance(part_x - line_x, part_y - line_y)
                        part_acc = part_acc + value * line_w
                        backward = value * part_w
                        totals[step] = totals[step] + jnp.sum(
                            backward.reshape(CHUNK // 8, 8, LANES), axis=0
                        )
                    own_acc[slot + 1, part, :] = part_acc
                for step in range(width):
                    other_acc[first + step] = totals[step]

            ends = tile + 1 >= own_tiles
            next_buffer = jnp.where(ends, 1 - buffer, buffer)
            next_tile = jnp.where(ends, 0, tile + 1)

            def first_body(width):
                close_tile(slot, last_group, last_line, last_tile)
                spread_out(next_buffer, next_tile, slot + 1)
                body(0, width, True)

            odd = other_tiles & 1

            @pl.when(odd == 1)
            def _():
                first_body(1)

            @pl.when(odd == 0)
            def _():
                first_body(2)

            def two(pair, nested):
                body(pair * 2 + odd, 2, False)
                return nested

            lax.fori_loop(1 - odd, lax.shift_right_logical(other_tiles, 1), two, 0)
            return own_group, own_line, tile

        last = lax.fori_loop(0, own_tiles, own_tile, (last_group, last_line, last_tile))
        start = start + own_tiles
        wrap = start > tiles

        @pl.when(wrap)
        def _():
            own_wide[0] = own_wide[start]
            own_acc[0] = own_acc[start]

        sums[other_group, other_line] += jnp.sum(other_acc[...], axis=1)
        other_acc[...] = jnp.zeros_like(other_acc)
        return jnp.where(wrap, 0, start), *last

    other_acc[...] = jnp.zeros_like(other_acc)
    own_acc[0] = jnp.zeros_like(own_acc[0])
    set_up(0, 0)
    spread_out(0, 0, 0)
    start, last_group, last_line, last_tile = lax.fori_loop(0, total, one_pair, (0, 0, 0, 0))
    close_tile(start, last_group, last_line, last_tile)


def step_kernel(
    row_count, col_count, sum_ref, meta_ref, spread_ref, var_ref, dir_ref, res_ref,
    iter_ref, iter_out, res_out, dir_out, row_land, col_land, stats, mine_stats,
    send_row, recv_row, send_col, recv_col, send_stat, recv_stat,
):
    my_row, my_col = lax.axis_index("rows"), lax.axis_index("cols")
    device_count = row_count * col_count
    me = my_row * col_count + my_col
    row_peers = [lax.rem(my_row + step, row_count) for step in range(1, row_count)]
    col_peers = [lax.rem(my_col + step, col_count) for step in range(1, col_count)]
    peers = others(row_count, col_count)
    barrier = greet_all(peers)
    local_rows = spread_ref.shape[0]
    meta = meta_ref[me]
    line_at = lax.broadcasted_iota(jnp.int32, spread_ref.shape, 0)
    counts = jnp.zeros(spread_ref.shape, jnp.int32)
    for line in range(local_rows):
        counts = jnp.where(line_at == line, meta[:, 2 * line : 2 * line + 1][None], counts)
    live = slot_numbers(spread_ref.shape) < counts
    masked_dir = jnp.where(live, dir_ref[...], 0.0)
    masked_res = jnp.where(live, res_ref[...], 0.0)
    pl.semaphore_wait(barrier, device_count - 1)

    copies = []
    for peer in row_peers:
        copies.append((col_count, col_land, my_row, peer, send_row, recv_row, "rows"))
    for peer in col_peers:
        copies.append((0, row_land, my_col, peer, send_col, recv_col, "cols"))
    for base, dst, mine, peer, sends, recvs, axis in copies:
        src = sum_ref.at[base + peer]
        remote(src, dst.at[mine], sends.at[peer], recvs.at[mine], {axis: peer}).start()
    total = sum_ref[my_col] + sum_ref[col_count + my_row]
    for base, dst, mine, peer, sends, recvs, axis in copies:
        src = sum_ref.at[base + peer]
        landed = remote(src, dst.at[peer], sends.at[peer], recvs.at[peer], {axis: peer})
        landed.wait_send()
        landed.wait_recv()
        total = total + dst[peer]

    image = jnp.where(live, spread_ref[...] * total + var_ref[...] * masked_dir, 0.0)

    def lane_sum(values):
        return jnp.sum(jnp.sum(values, axis=0), axis=0, keepdims=True)

    for index, values in enumerate(
        (masked_res * masked_res, masked_dir * image, masked_res * image, image * image)
    ):
        mine_stats[pl.ds(index, 1), :] = lane_sum(values)
    stats[me] = mine_stats[...]

    for peer in peers:
        remote(mine_stats, stats.at[me], send_stat, recv_stat, peer).start()
    every = stats.at[pl.ds(0, device_count - 1)]
    pltpu.make_async_copy(every, every, send_stat).wait()
    pltpu.make_async_copy(every, every, recv_stat).wait()
    sums = jnp.sum(jnp.sum(stats[...], axis=0), axis=1, keepdims=True)
    res_norm, curvature, cross, image_norm = (sums[at : at + 1, :][None] for at in range(4))
    step_size = res_norm / curvature
    next_norm = res_norm - 2.0 * step_size * cross + step_size * step_size * image_norm
    residual_next = masked_res - step_size * image
    iter_out[...] = jnp.where(live, iter_ref[...], 0.0) + step_size * masked_dir
    res_out[...] = residual_next
    dir_out[...] = residual_next + next_norm / res_norm * masked_dir


def vmem(count):
    return [pl.BlockSpec(memory_space=pltpu.VMEM)] * count


def local(
    row_count, col_count, positions, region_cell, spread, obs_var, counts, pair_flags, iterate,
    residual, direction,
):
    local_rows, _, slots = spread.shape
    tiles = slots // LANES
    flat = (local_rows, tiles, LANES)
    device_count = row_count * col_count
    f32, i32 = jnp.float32, jnp.int32
    dma = pltpu.SemaphoreType.DMA
    spread_l, var_l, iter_l, res_l, dir_l = (
        value.reshape(flat) for value in (spread, obs_var, iterate, residual, direction)
    )
    grid_cells = device_count * local_rows
    row_part, col_part, meta = pl.pallas_call(
        functools.partial(gather_kernel, row_count, col_count),
        out_shape=(
            jax.ShapeDtypeStruct((col_count, 3, local_rows, tiles, LANES), f32),
            jax.ShapeDtypeStruct((row_count, 3, local_rows, tiles, LANES), f32),
            jax.ShapeDtypeStruct((device_count, 1, LANES), i32),
        ),
        in_specs=[pl.BlockSpec(memory_space=pltpu.HBM)] * 3,
        out_specs=tuple(vmem(3)),
        scratch_shapes=[
            pltpu.VMEM((local_rows, 4, slots), f32),
            pltpu.VMEM((1, local_rows), i32),
            pltpu.VMEM((1, local_rows), i32),
            dma((3,)),
            dma((row_count,)),
            dma((row_count,)),
            dma((col_count,)),
            dma((col_count,)),
            dma(()),
            dma(()),
        ],
        compiler_params=pltpu.CompilerParams(
            collective_id=0, has_side_effects=True, vmem_limit_bytes=VMEM_BYTES
        ),
        name="gather_parts",
    )(
        jnp.concatenate([positions.reshape(local_rows, 2, slots), spread, direction], axis=1),
        region_cell.reshape(1, local_rows),
        counts.reshape(1, local_rows),
    )

    sums = pl.pallas_call(
        pair_kernel,
        out_shape=jax.ShapeDtypeStruct((col_count + row_count, local_rows, tiles, LANES), f32),
        in_specs=[pl.BlockSpec(memory_space=pltpu.SMEM)] + vmem(2),
        out_specs=vmem(1)[0],
        scratch_shapes=[
            pltpu.VMEM((2 * tiles + 1, 3, LANES, LANES), f32),
            pltpu.VMEM((2 * tiles + 1, LANES, LANES), f32),
            pltpu.VMEM((tiles, 8, LANES), f32),
            pltpu.VMEM((2, 3, tiles, LANES), f32),
            pltpu.VMEM((2, 3, tiles, LANES), f32),
        ]
        + [pltpu.SMEM((grid_cells + col_count,), i32)] * 4
        + [pltpu.SMEM((device_count,), i32), pltpu.SMEM((5 * grid_cells + 1,), i32)],
        compiler_params=pltpu.CompilerParams(vmem_limit_bytes=VMEM_BYTES),
        name="pair_sums",
    )(meta.reshape(device_count, LANES), row_part, col_part)

    outs = pl.pallas_call(
        functools.partial(step_kernel, row_count, col_count),
        out_shape=(jax.ShapeDtypeStruct(flat, f32),) * 3,
        in_specs=vmem(7),
        out_specs=tuple(vmem(3)),
        scratch_shapes=[
            pltpu.VMEM((col_count, local_rows, tiles, LANES), f32),
            pltpu.VMEM((row_count, local_rows, tiles, LANES), f32),
            pltpu.VMEM((device_count, 4, LANES), f32),
            pltpu.VMEM((4, LANES), f32),
            dma((row_count,)),
            dma((row_count,)),
            dma((col_count,)),
            dma((col_count,)),
            dma(()),
            dma(()),
        ],
        compiler_params=pltpu.CompilerParams(
            collective_id=1, has_side_effects=True, vmem_limit_bytes=VMEM_BYTES
        ),
        name="reduce_and_step",
    )(sums, meta, spread_l, var_l, dir_l, res_l, iter_l)
    return tuple(out.reshape(spread.shape) for out in outs)


def solution(mesh):
    per_slot = P(("groups", "rows"), "cols", None)
    return jax.shard_map(
        functools.partial(local, mesh.shape["rows"], mesh.shape["cols"]),
        mesh=mesh,
        in_specs=(
            P(("groups", "rows"), "cols", None, None),
            P(("groups", "rows"), "cols"),
            per_slot,
            per_slot,
            P(("groups", "rows"), "cols"),
            P(("groups", "rows"), None, None, "cols"),
            per_slot,
            per_slot,
            per_slot,
        ),
        out_specs=(per_slot, per_slot, per_slot),
        check_vma=False,
    )
```
